32 devices in a mesh: sec: 2 (over core), req: 4 (over z), kv: 4 (over y, x).
Axes of the slice: x: 2, y: 2, z: 4, core: 2. Of those that a mesh axis runs over, the one named last changes fastest.
Arguments:
- queries: bfloat16 [512, 4096], P('req', ('kv', 'sec')), may hold values from -21 to 21
- key_cache: bfloat16 [512, 4, 32, 128], P('req', 'kv'), may hold values from -21 to 21
- value_cache: bfloat16 [512, 4, 32, 128], P('req', 'kv'), may hold values from -18 to 18
- new_keys: bfloat16 [512, 4, 128], P('req', 'kv'), may hold values from -5 to 5
- new_values: bfloat16 [512, 4, 128], P('req', 'kv'), may hold values from -18 to 18
- lengths: int32 [512], P('req'), may hold values from 2 to 32
- out_proj: bfloat16 [4096, 4096], P(('kv', 'sec')), may hold values from -0.09375 to 0.09375
- residual: bfloat16 [512, 4096], P(('req', 'sec', 'kv')), may hold values from -36 to 36
- norm_gain: float32 [4096], replicated, may hold values from 0.1 to 1.9
- expert_ids: int32 [512, 8], P(('req', 'sec', 'kv')), may hold values from 0 to 31, as said below
- expert_slots: int32 [512, 8], P(('req', 'sec', 'kv')), may hold values from 0 to 4, as said below
- gate_probs: float32 [512, 8], P(('req', 'sec', 'kv')), may hold values from 0.1 to 0.4
- w_gate: bfloat16 [32, 4096, 768], P(('sec', 'req', 'kv')), may hold values from -0.09375 to 0.09375
- w_up: bfloat16 [32, 4096, 768], P(('sec', 'req', 'kv')), may hold values from -0.09375 to 0.09375
- w_down: bfloat16 [32, 768, 4096], P(('sec', 'req', 'kv')), may hold values from -0.21875 to 0.21875
Outputs:
- stream: bfloat16 [512, 4096], P(('req', 'sec', 'kv'))
- moe_out: bfloat16 [512, 4096], P(('req', 'sec', 'kv'))
The draws below stay inside these ranges and needn't reach their ends.
Inputs may be any that keep to these rules, and one draw needn't show every extreme that they name: `expert_ids`: each row names 8 different experts. In each block of 16 consecutive rows (the rows of one device) every expert is named at least 3 and at most 5 times, and one expert, the same for all blocks, exactly 5 times. `expert_slots`: within a block the entries naming one expert hold different slots, numbered from 0 in row order.
All inputs are finite; a program needn't handle non-finite values.
Results may differ from the reference program's by a relative error of at most 0.029.
Values may be sent and summed in bfloat16 or wider, within the bound.
A program may use at most 128 MiB of HBM per device.

```python
import jax
import jax.numpy as jnp
from jax import lax

D = 4096
HD = 128
QH = 32
KVH = 4
FFW = 768
TOPK = 8
CTX = 32
TOKENS = 512
EXPERTS = 32
BLOCK = 16
ROUNDS = 4
CAP = 5


def cache_base(key):
    return jnp.clip(jax.random.normal(key, (TOKENS, KVH, CTX, HD), jnp.float32), -4.0, 4.0)


def route_tables(key):
    block_total = TOKENS // BLOCK
    hot_expert = jax.random.randint(jax.random.fold_in(key, 7001), (), 0, EXPERTS)
    extras = jax.random.randint(jax.random.fold_in(key, 7002), (block_total,), 1, EXPERTS // 2 + 1)
    full_block = jax.random.randint(jax.random.fold_in(key, 7003), (), 0, block_total)
    extras = jnp.where(jnp.arange(block_total) == full_block, EXPERTS // 2, extras).astype(jnp.int32)

    def one_block(block_number, extra):
        block_key = jax.random.fold_in(key, block_number)
        order = jax.random.permutation(jax.random.fold_in(block_key, 1), EXPERTS).astype(jnp.int32)
        position_hot = jnp.argmax(order == hot_expert)
        order = order.at[position_hot].set(order[0]).at[0].set(hot_expert)
        rank = jnp.arange(EXPERTS, dtype=jnp.int32)
        counts = ROUNDS + (rank < extra).astype(jnp.int32) - ((rank >= extra) & (rank < 2 * extra)).astype(jnp.int32)
        ends = jnp.cumsum(counts)
        flat = jnp.arange(BLOCK * TOPK, dtype=jnp.int32)
        which = jnp.sum((ends[None, :] <= flat[:, None]).astype(jnp.int32), axis=1)
        entries = order[which]
        grid = entries.reshape(TOPK, BLOCK).T
        row_order = jax.random.permutation(jax.random.fold_in(block_key, 2), BLOCK)
        grid = grid[row_order]
        column_order = jax.vmap(lambda row_number: jax.random.permutation(jax.random.fold_in(block_key, 100 + row_number), TOPK))(jnp.arange(BLOCK))
        grid = jnp.take_along_axis(grid, column_order, axis=1)
        listed = grid.reshape(-1)
        one_hot = (listed[:, None] == jnp.arange(EXPERTS, dtype=jnp.int32)[None, :]).astype(jnp.int32)
        earlier = jnp.cumsum(one_hot, axis=0) - one_hot
        slot_numbers = jnp.sum(earlier * one_hot, axis=1)
        return (grid, slot_numbers.reshape(BLOCK, TOPK))
    ids_table, slot_table = jax.vmap(one_block)(jnp.arange(block_total), extras)
    return (ids_table.reshape(TOKENS, TOPK).astype(jnp.int32), slot_table.reshape(TOKENS, TOPK).astype(jnp.int32))


def draw_expert_ids(key, part):
    ids_table, slot_table = route_tables(key)
    return ids_table


def draw_expert_slots(key, part):
    ids_table, slot_table = route_tables(key)
    return slot_table


def draw_key_cache(key, part):
    shared = cache_base(key)
    return shared.astype(jnp.bfloat16)


def draw_queries(key, part):
    key = jax.random.fold_in(key, 41)
    drawn = jnp.clip(jax.random.normal(key, (TOKENS, QH * HD), jnp.float32), -4.0, 4.0)
    return drawn.astype(jnp.bfloat16)


def draw_residual(key, part):
    key = jax.random.fold_in(key, 51)
    base_key, row_key, column_key = jax.random.split(key, 3)
    base = jnp.clip(jax.random.normal(base_key, (TOKENS, D), jnp.float32), -4.0, 4.0)
    low_end = jnp.log(0.3)
    high_end = jnp.log(3.0)
    row_scale = jnp.exp(jax.random.uniform(row_key, (TOKENS, 1), jnp.float32, low_end, high_end))
    column_scale = jnp.exp(jax.random.uniform(column_key, (1, D), jnp.float32, low_end, high_end))
    return (base * row_scale * column_scale).astype(jnp.bfloat16)


def plant(array, key, smallest, high):
    index_at = [jax.random.randint(jax.random.fold_in(key, axis), (), 0, length) for axis, length in enumerate(array.shape)]
    main_axis = array.shape.index(max(array.shape))
    next_to = index_at[:main_axis] + [(index_at[main_axis] + 1) % array.shape[main_axis]] + index_at[main_axis + 1:]
    return array.at[tuple(index_at)].set(smallest).at[tuple(next_to)].set(high)


def block_levels(key, dims, pieces, low, largest):
    loudness = 1.0
    for dim, shards_of in pieces:
        draws = jax.random.uniform(jax.random.fold_in(jax.random.fold_in(key, 6), dim), (shards_of,), jnp.float32, low / len(pieces), largest / len(pieces))
        loudness = loudness * jnp.repeat(jnp.exp(draws), dims[dim] // shards_of).reshape((-1,) + (1,) * (len(dims) - 1 - dim))
    return loudness


def bell_draw(own_key, dims, scale, most, shards=(), kind=jnp.bfloat16):
    level = block_levels(own_key, dims, shards, -0.22, 0.18) if shards else 1.0
    values = jax.random.normal(own_key, dims, jnp.float32) * scale * level
    return jnp.minimum(jnp.maximum(values, -most), most).astype(kind)


def setup_inputs(seed: int = 0) -> dict:
    arg_keys = jax.random.split(jax.random.key(seed), 16)
    queries = draw_queries(jax.random.fold_in(arg_keys[15], 71), 0)
    key_cache = draw_key_cache(jax.random.fold_in(arg_keys[15], 71), 0)
    value_cache = bell_draw(arg_keys[2], (TOKENS, KVH, CTX, HD), 3.0, 18.0, ((0, 4), (1, 4)))
    new_keys = bell_draw(arg_keys[3], (TOKENS, KVH, HD), 1.0, 5.0, ((0, 4), (1, 4)))
    new_values = bell_draw(arg_keys[4], (TOKENS, KVH, HD), 3.0, 18.0, ((0, 4), (1, 4)))
    lengths = plant(jax.random.randint(arg_keys[5], (TOKENS,), 2, CTX + 1), jax.random.fold_in(arg_keys[5], 1), 2, CTX).astype(jnp.int32)
    out_proj = bell_draw(arg_keys[6], (QH * HD, D), (QH * HD) ** -0.5, 0.09375, ((0, 8),))
    residual = draw_residual(jax.random.fold_in(arg_keys[15], 71), 0)
    norm_gain = jnp.clip(1.0 + 0.18 * jax.random.normal(arg_keys[8], (D,), jnp.float32), 0.1, 1.9)
    expert_ids = draw_expert_ids(jax.random.fold_in(arg_keys[15], 71), 0)
    expert_slots = draw_expert_slots(jax.random.fold_in(arg_keys[15], 71), 0)
    gate_probs = jnp.clip(0.1 + 0.3 * jax.random.uniform(arg_keys[11], (TOKENS, TOPK), jnp.float32) ** block_levels(arg_keys[11], (TOKENS, TOPK), ((0, 32),), -0.2, 0.2), 0.1, 0.4)
    w_gate = bell_draw(arg_keys[12], (EXPERTS, D, FFW), D ** -0.5, 0.09375, ((0, 32),))
    w_up = bell_draw(arg_keys[13], (EXPERTS, D, FFW), D ** -0.5, 0.09375, ((0, 32),))
    w_down = bell_draw(arg_keys[14], (EXPERTS, FFW, D), FFW ** -0.5, 0.21875, ((0, 32),))
    return {"queries": queries, "key_cache": key_cache, "value_cache": value_cache, "new_keys": new_keys, "new_values": new_values, "lengths": lengths, "out_proj": out_proj, "residual": residual, "norm_gain": norm_gain, "expert_ids": expert_ids, "expert_slots": expert_slots, "gate_probs": gate_probs, "w_gate": w_gate, "w_up": w_up, "w_down": w_down}


def run_expert(operands):
    rows_in, gate_weight, up_weight, down_weight = operands
    gate_out = jnp.dot(rows_in, gate_weight, preferred_element_type=jnp.float32)
    up_out = jnp.dot(rows_in, up_weight, preferred_element_type=jnp.float32)
    hidden = (jax.nn.silu(gate_out) * up_out).astype(jnp.bfloat16)
    return jnp.dot(hidden, down_weight, preferred_element_type=jnp.float32).astype(jnp.bfloat16)

def reference(queries, key_cache, value_cache, new_keys, new_values, lengths, out_proj, residual, norm_gain, expert_ids, expert_slots, gate_probs, w_gate, w_up, w_down):
    group = QH // KVH
    score_scale = 1.0 / HD ** 0.5
    query_heads = queries.astype(jnp.float32).reshape(TOKENS, KVH, group, HD)
    score = jnp.einsum('tghd,tgpd->tghp', query_heads, key_cache.astype(jnp.float32)) * score_scale
    own_score = jnp.einsum('tghd,tgd->tgh', query_heads, new_keys.astype(jnp.float32)) * score_scale
    valid = jnp.arange(CTX, dtype=jnp.int32)[None, :] < lengths[:, None]
    score = jnp.where(valid[:, None, None, :], score, -jnp.inf)
    highest = jnp.maximum(lax.optimization_barrier(jnp.max(score, axis=-1)), own_score)
    raised = jnp.exp(score - highest[..., None])
    own_raised = jnp.exp(own_score - highest)
    denominator = lax.optimization_barrier(jnp.sum(raised, axis=-1)) + own_raised
    weight = (raised / denominator[..., None]).astype(jnp.bfloat16)
    own_weight = (own_raised / denominator).astype(jnp.bfloat16)
    attn = jnp.einsum('tghp,tgpd->tghd', weight.astype(jnp.float32), value_cache.astype(jnp.float32))
    attn = attn + own_weight.astype(jnp.float32)[..., None] * new_values.astype(jnp.float32)[:, :, None, :]
    attn = attn.astype(jnp.bfloat16).reshape(TOKENS, QH * HD)
    proj = jnp.dot(attn, out_proj, preferred_element_type=jnp.float32)
    stream = (residual.astype(jnp.float32) + proj).astype(jnp.bfloat16)
    widened = lax.optimization_barrier(stream).astype(jnp.float32)
    mean_square = lax.optimization_barrier(jnp.mean(widened * widened, axis=-1, keepdims=True))
    normed = (widened * lax.rsqrt(mean_square + 1e-06) * norm_gain).astype(jnp.bfloat16)
    block_count = TOKENS // BLOCK
    block_of = (jnp.arange(TOKENS, dtype=jnp.int32) // BLOCK)[:, None]
    slot_index = (expert_ids * (block_count * CAP) + block_of * CAP + expert_slots).astype(jnp.int32).reshape(-1)
    repeated = jnp.broadcast_to(normed[:, None, :], (TOKENS, TOPK, D)).reshape(TOKENS * TOPK, D)
    expert_in = jnp.zeros((EXPERTS * block_count * CAP, D), jnp.bfloat16).at[slot_index].set(repeated)
    expert_in = expert_in.reshape(EXPERTS, block_count * CAP, D)
    expert_out = lax.map(run_expert, (expert_in, w_gate, w_up, w_down))
    picked = expert_out.reshape(EXPERTS * block_count * CAP, D)[slot_index].reshape(TOKENS, TOPK, D)
    moe_out = lax.optimization_barrier(jnp.sum(picked.astype(jnp.float32) * gate_probs[..., None], axis=1)).astype(jnp.bfloat16)
    return (stream, moe_out)
```

```python
import functools

import jax
import jax.numpy as jnp
import numpy as np
from jax import lax
from jax.experimental import pallas as pl
from jax.experimental.pallas import tpu as pltpu
from jax.sharding import PartitionSpec as P

MESH = pl.DeviceIdType.MESH
CHUNKS = 4
BF16 = jnp.bfloat16
F32 = jnp.float32


def dot(a, b):
    return jnp.dot(a, b, preferred_element_type=F32)


def layout(blocks, capacity):
    slots = blocks * capacity
    left = slots - 16
    if left in (1, 2, 4, 8):
        return 16, left
    return -(-slots // 16) * 16, 0


def layer_kernel(
    dims,
    attn_ref,
    out_proj_hbm,
    residual_ref,
    gain_ref,
    table_ref,
    col_ref,
    col_left_ref,
    row_ref,
    row_left_ref,
    unpack_ref,
    pack_ref,
    gate_hbm,
    up_hbm,
    down_hbm,
    stream_ref,
    moe_ref,
    out_proj,
    w_gate,
    w_up,
    w_down,
    sib_out,
    sib_in,
    part_out,
    part_in,
    tables,
    pick,
    pick_left,
    spread,
    spread_left,
    tokens,
    disp_out,
    disp_in,
    rows_in,
    gate_acc,
    up_acc,
    ret_out,
    ret_in,
    sum_out,
    sum_in,
    weight_sem,
    sib_sem,
    part_sem,
    table_sem,
    token_sem,
    disp_sem,
    ret_sem,
    sum_sem,
):
    R, K, full, left = dims["R"], dims["K"], dims["full"], dims["left"]
    top = dims["top"]
    M = 2 * K
    nch = CHUNKS
    width = stream_ref.shape[1]
    cw = width // nch
    parts = 16 // left if left else 0
    lw = cw // parts if left else 0
    s = lax.axis_index("sec")
    r = lax.axis_index("req")
    k = lax.axis_index("kv")
    m = s * K + k

    def cols(j):
        return pl.ds(pl.multiple_of(j * cw, cw), cw)

    def weight_copy(which, j):
        src, dst = [
            (out_proj_hbm.at[:, cols(j)], out_proj),
            (gate_hbm.at[0, cols(j)], w_gate),
            (up_hbm.at[0, cols(j)], w_up),
            (down_hbm.at[0, :, cols(j)], w_down),
        ][which]
        return pltpu.make_async_copy(src, dst.at[j], weight_sem.at[which, j])

    for which in range(4):
        for j in range(nch):
            weight_copy(which, j).start()

    def line(i):
        return lax.rem(r + i, R)

    def plane(i):
        return lax.rem(m + i, M)

    def remote(src, dst, sems, at, device):
        return pltpu.make_async_remote_copy(
            src_ref=src,
            dst_ref=dst,
            send_sem=sems.at[(0, *at)],
            recv_sem=sems.at[(1, *at)],
            device_id=device,
            device_id_type=MESH,
        )

    barrier = pltpu.get_barrier_semaphore()
    for i in range(1, M):
        p = plane(i)
        pl.semaphore_signal(
            barrier, inc=1, device_id=(p // K, r, lax.rem(p, K)), device_id_type=MESH
        )
    for i in range(1, R):
        pl.semaphore_signal(barrier, inc=1, device_id=(s, line(i), k), device_id_type=MESH)
    pl.semaphore_wait(barrier, M + R - 2)

    def table_copy(i, me):
        return remote(table_ref, tables.at[me], table_sem, (i - 1,), (s, line(i), k))

    def sib_copy(j):
        return remote(sib_out.at[j], sib_in.at[j], sib_sem, (j,), (1 - s, r, k))

    def part_copy(j, i):
        to = lax.rem(k + i, K)
        return remote(
            part_out.at[j, to], part_in.at[j, i - 1], part_sem, (j, i - 1), (s, r, to)
        )

    def token_copy(j, i, me):
        return remote(tokens.at[j, me], tokens.at[j, me], token_sem, (j, i - 1), (s, line(i), k))

    def plane_copy(out, into, sems, j, i, me):
        p = plane(i)
        return remote(out.at[j, p], into.at[j, me], sems, (j, i - 1), (p // K, r, lax.rem(p, K)))

    def sum_copy(j, i):
        to = line(i)
        return remote(sum_out.at[j, to], sum_in.at[j, i - 1], sum_sem, (j, i - 1), (s, to, k))

    def before(i):
        return lax.rem(r - i + R, R)

    def plane_before(i):
        return lax.rem(m - i + M, M)

    for i in range(1, R):
        table_copy(i, r).start()
    tables[r] = table_ref[...]

    @pl.loop(0, nch)
    def _(j):
        weight_copy(0, j).wait()
        sib_out[j] = dot(attn_ref[1 - s], out_proj[j]).astype(BF16)
        sib_copy(j).start()

    @pl.loop(0, nch)
    def _(j):
        own = dot(attn_ref[s], out_proj[j])
        sib_copy(j).wait_recv()
        part_out[j] = (own + sib_in[j].astype(F32)).astype(BF16).reshape(K, 16, cw)
        for i in range(1, K):
            part_copy(j, i).start()

    for i in range(1, R):
        table_copy(i, before(i)).wait_recv()
    codes = tables[0, 0:top, :]
    for q in range(1, R):
        codes = jnp.maximum(codes, tables[q, 0:top, :])
    codes = codes[:, : R * 16]

    def one_hot(targets):
        total = jnp.zeros((targets.shape[0], R * 16), F32)
        for n in range(top):
            total = total + jnp.where(codes[n : n + 1, :] == targets, 1.0, 0.0)
        return total.astype(BF16)

    def weighted(q, targets):
        total = jnp.zeros((16, targets.shape[1]), F32)
        entry = tables[q, top : top + 16, :]
        for n in range(top):
            total = total + jnp.where(
                entry[:, n : n + 1] == targets, entry[:, top + n : top + n + 1], 0.0
            )
        return total.astype(BF16)

    pick[...] = one_hot(col_ref[...])
    for q in range(parts):
        pick_left[q] = one_hot(col_left_ref[q])
    for q in range(R):
        spread[q * 16 : (q + 1) * 16, :] = weighted(q, row_ref[...])
        for n in range(parts):
            spread_left[n, q * 16 : (q + 1) * 16, :] = weighted(q, row_left_ref[n])

    def add_parts(j, squares):
        total = part_out[j, k].astype(F32)
        for i in range(1, K):
            part_copy(j, i).wait_recv()
            total = total + part_in[j, i - 1].astype(F32)
        value = (residual_ref[:, cols(j)].astype(F32) + total).astype(BF16)
        stream_ref[:, cols(j)] = value
        value = value.astype(F32)
        return squares + jnp.sum(value * value, axis=1, keepdims=True)

    squares = lax.fori_loop(0, nch, add_parts, jnp.zeros((16, 1), F32))
    scale = lax.rsqrt(squares * (1.0 / width) + 1e-06)

    @pl.loop(0, nch)
    def _(j):
        value = stream_ref[:, cols(j)].astype(F32)
        tokens[j, r] = (value * scale * gain_ref[:, cols(j)]).astype(BF16)
        for i in range(1, R):
            token_copy(j, i, r).start()

    @pl.loop(0, nch)
    def _(j):
        for i in range(1, R):
            token_copy(j, i, before(i)).wait_recv()
        held = tokens[j].reshape(R * 16, cw)
        disp_out[j, :, :, 0:cw] = dot(pick[...], held).astype(BF16).reshape(M, full, cw)
        if left:
            extra = dot(pick_left[0], held[:, 0:lw])
            for q in range(1, parts):
                extra = extra + dot(pick_left[q], held[:, q * lw : (q + 1) * lw])
            disp_out[j, :, :, cw : cw + lw] = extra.astype(BF16).reshape(M, 16, lw)
        for i in range(1, M):
            plane_copy(disp_out, disp_in, disp_sem, j, i, m).start()
        disp_in[j, m] = disp_out[j, m]

    gate_acc[...] = jnp.zeros_like(gate_acc)
    up_acc[...] = jnp.zeros_like(up_acc)

    @pl.loop(0, nch)
    def _(j):
        weight_copy(1, j).wait()
        weight_copy(2, j).wait()
        for i in range(1, M):
            plane_copy(disp_out, disp_in, disp_sem, j, i, plane_before(i)).wait_recv()
        rows_in[0 : M * full, :] = disp_in[j, :, :, 0:cw].reshape(M * full, cw)
        if left:
            extra = disp_in[j, :, :, cw : cw + lw].reshape(M * 16, lw)
            for q in range(parts):
                rows_in[M * full :, q * lw : (q + 1) * lw] = dot(unpack_ref[q], extra).astype(BF16)
        gate_acc[...] += dot(rows_in[...], w_gate[j])
        up_acc[...] += dot(rows_in[...], w_up[j])

    gate_out = gate_acc[...]
    hidden = (gate_out / (1.0 + jnp.exp(-gate_out)) * up_acc[...]).astype(BF16)

    @pl.loop(0, nch)
    def _(j):
        weight_copy(3, j).wait()
        finished = dot(hidden, w_down[j]).astype(BF16)
        ret_out[j, :, :, 0:cw] = finished[0 : M * full].reshape(M, full, cw)
        if left:
            rest = finished[M * full :]
            extra = dot(pack_ref[0], rest[:, 0:lw])
            for q in range(1, parts):
                extra = extra + dot(pack_ref[q], rest[:, q * lw : (q + 1) * lw])
            ret_out[j, :, :, cw : cw + lw] = extra.astype(BF16).reshape(M, 16, lw)
        for i in range(1, M):
            plane_copy(ret_out, ret_in, ret_sem, j, i, m).start()
        ret_in[j, m] = ret_out[j, m]

    @pl.loop(0, nch)
    def _(j):
        for i in range(1, M):
            plane_copy(ret_out, ret_in, ret_sem, j, i, plane_before(i)).wait_recv()
        total = dot(spread[...], ret_in[j, :, :, 0:cw].reshape(M * full, cw))
        if left:
            extra = ret_in[j, :, :, cw : cw + lw].reshape(M * 16, lw)
            total = total + jnp.concatenate(
                [dot(spread_left[q], extra) for q in range(parts)], axis=1
            )
        sum_out[j] = total.astype(BF16).reshape(R, 16, cw)
        for i in range(1, R):
            sum_copy(j, i).start()

    @pl.loop(0, nch)
    def _(j):
        total = sum_out[j, r].astype(F32)
        for i in range(1, R):
            sum_copy(j, i).wait_recv()
            total = total + sum_in[j, i - 1].astype(F32)
        moe_ref[:, cols(j)] = total.astype(BF16)

    for i in range(1, R):
        table_copy(i, r).wait_send()

    @pl.loop(0, nch)
    def _(j):
        sib_copy(j).wait_send()
        for i in range(1, K):
            part_copy(j, i).wait_send()
        for i in range(1, R):
            token_copy(j, i, r).wait_send()
            sum_copy(j, i).wait_send()
        for i in range(1, M):
            plane_copy(disp_out, disp_in, disp_sem, j, i, m).wait_send()
            plane_copy(ret_out, ret_in, ret_sem, j, i, m).wait_send()


def attention(queries, key_cache, value_cache, new_keys, new_values, lengths):
    row_count, head_width = queries.shape
    head_size = key_cache.shape[3]
    positions = key_cache.shape[2]
    heads_here = head_width // head_size
    score_scale = 1.0 / head_size**0.5
    query_heads = queries.reshape(row_count, heads_here, head_size)
    score = (
        jnp.einsum("thd,tpd->thp", query_heads, key_cache[:, 0], preferred_element_type=F32)
        * score_scale
    )
    own_score = (
        jnp.einsum("thd,td->th", query_heads, new_keys[:, 0], preferred_element_type=F32)
        * score_scale
    )
    valid = jnp.arange(positions, dtype=jnp.int32)[None, :] < lengths[:, None]
    score = jnp.where(valid[:, None, :], score, -jnp.inf)
    highest = jnp.maximum(jnp.max(score, axis=-1), own_score)
    raised = jnp.exp(score - highest[..., None])
    own_raised = jnp.exp(own_score - highest)
    denominator = jnp.sum(raised, axis=-1) + own_raised
    weight = (raised / denominator[..., None]).astype(BF16)
    own_weight = (own_raised / denominator).astype(BF16)
    attn = jnp.einsum("thp,tpd->thd", weight, value_cache[:, 0], preferred_element_type=F32)
    attn = attn + own_weight.astype(F32)[..., None] * new_values[:, 0].astype(F32)[:, None, :]
    return attn.astype(BF16).reshape(row_count, head_width)


def on_device(
    queries,
    key_cache,
    value_cache,
    new_keys,
    new_values,
    lengths,
    out_proj,
    residual,
    norm_gain,
    expert_ids,
    expert_slots,
    gate_probs,
    w_gate,
    w_up,
    w_down,
):
    attn = attention(queries, key_cache, value_cache, new_keys, new_values, lengths)
    R, K = lax.axis_size("req"), lax.axis_size("kv")
    M = 2 * K
    experts = R * M
    block, top = expert_ids.shape
    width = out_proj.shape[1]
    depth = out_proj.shape[0]
    hidden_units = w_gate.shape[2]
    capacity = top * block // experts + 1
    full, left = layout(R, capacity)
    parts = 16 // left if left else 1
    nch = CHUNKS
    cw = width // nch
    total_width = cw + (cw // parts if left else 0)
    r = lax.axis_index("req")

    codes = (r * (experts * capacity) + expert_ids * capacity + expert_slots).astype(F32)
    lanes = -(-R * block // 128) * 128
    by_lane = lax.dynamic_update_slice(
        jnp.full((top, lanes), -1.0, F32), codes.T, (jnp.int32(0), r * block)
    )
    by_row = jnp.pad(
        jnp.concatenate([codes, gate_probs], axis=1), ((0, 0), (0, lanes - 2 * top))
    )
    table = jnp.concatenate([by_lane, by_row], axis=0)

    member = np.arange(M)
    base = ((member // K) * R * K + member % K) * capacity
    slot = np.arange(full)
    code_of = (slot // capacity) * (experts * capacity) + slot % capacity
    targets = base[:, None] + np.where(slot < R * capacity, code_of, -(10**6))[None, :]
    targets = targets.reshape(-1).astype(np.float32)
    left_targets = np.full((parts, M, 16), -(10.0**6), np.float32)
    unpack = np.zeros((parts, M * max(left, 1), M * 16), np.float32)
    for q in range(parts if left else 0):
        for n in range(left):
            sigma = full + n
            code = (sigma // capacity) * (experts * capacity) + sigma % capacity
            left_targets[q, :, q * left + n] = base + code
            unpack[q, member * left + n, member * 16 + q * left + n] = 1.0
    shift = (r * (K * capacity)).astype(F32)
    targets = jnp.asarray(targets) + shift
    left_targets = jnp.asarray(left_targets.reshape(parts, M * 16)) + shift

    rows = M * (full + left)
    dims = {"R": R, "K": K, "full": full, "left": left, "top": top}
    vmem = pl.BlockSpec(memory_space=pltpu.VMEM)
    hbm = pl.BlockSpec(memory_space=pl.ANY)
    dma = pltpu.SemaphoreType.DMA
    outs = jax.ShapeDtypeStruct((block, width), BF16)
    return pl.pallas_call(
        functools.partial(layer_kernel, dims),
        out_shape=(outs, outs),
        in_specs=[vmem, hbm] + [vmem] * 9 + [hbm] * 3,
        out_specs=(vmem, vmem),
        scratch_shapes=[
            pltpu.VMEM((nch, depth, cw), BF16),
            pltpu.VMEM((nch, cw, hidden_units), BF16),
            pltpu.VMEM((nch, cw, hidden_units), BF16),
            pltpu.VMEM((nch, hidden_units, cw), BF16),
            pltpu.VMEM((nch, K * block, cw), BF16),
            pltpu.VMEM((nch, K * block, cw), BF16),
            pltpu.VMEM((nch, K, block, cw), BF16),
            pltpu.VMEM((nch, K - 1, block, cw), BF16),
            pltpu.VMEM((R, top + block, lanes), F32),
            pltpu.VMEM((M * full, R * block), BF16),
            pltpu.VMEM((parts, M * 16, R * block), BF16),
            pltpu.VMEM((R * block, M * full), BF16),
            pltpu.VMEM((parts, R * block, M * 16), BF16),
            pltpu.VMEM((nch, R, block, cw), BF16),
            pltpu.VMEM((nch, M, full, total_width), BF16),
            pltpu.VMEM((nch, M, full, total_width), BF16),
            pltpu.VMEM((rows, cw), BF16),
            pltpu.VMEM((rows, hidden_units), F32),
            pltpu.VMEM((rows, hidden_units), F32),
            pltpu.VMEM((nch, M, full, total_width), BF16),
            pltpu.VMEM((nch, M, full, total_width), BF16),
            pltpu.VMEM((nch, R, block, cw), BF16),
            pltpu.VMEM((nch, R - 1, block, cw), BF16),
            dma((4, nch)),
            dma((2, nch)),
            dma((2, nch, K - 1)),
            dma((2, R - 1)),
            dma((2, nch, R - 1)),
            dma((2, nch, M - 1)),
            dma((2, nch, M - 1)),
            dma((2, nch, R - 1)),
        ],
        compiler_params=pltpu.CompilerParams(
            collective_id=0, has_side_effects=True, vmem_limit_bytes=58 * 2**20
        ),
    )(
        attn.reshape(2, K * block, depth),
        out_proj,
        residual,
        norm_gain.reshape(1, width),
        table,
        targets.reshape(-1, 1),
        left_targets.reshape(parts, M * 16, 1),
        targets.reshape(1, -1),
        left_targets.reshape(parts, 1, M * 16),
        jnp.asarray(unpack, BF16),
        jnp.asarray(unpack.transpose(0, 2, 1), BF16),
        w_gate,
        w_up,
        w_down,
    )


def solution(mesh):
    return jax.shard_map(
        on_device,
        mesh=mesh,
        in_specs=(
            P("req", ("kv", "sec")),
            P("req", "kv", None, None),
            P("req", "kv", None, None),
            P("req", "kv", None),
            P("req", "kv", None),
            P("req"),
            P(("kv", "sec"), None),
            P(("req", "sec", "kv"), None),
            P(),
            P(("req", "sec", "kv"), None),
            P(("req", "sec", "kv"), None),
            P(("req", "sec", "kv"), None),
            P(("sec", "req", "kv"), None, None),
            P(("sec", "req", "kv"), None, None),
            P(("sec", "req", "kv"), None, None),
        ),
        out_specs=(P(("req", "sec", "kv"), None), P(("req", "sec", "kv"), None)),
        check_vma=False,
    )
```

```python
import functools

import jax
import jax.numpy as jnp
import numpy as np
from jax import lax
from jax.experimental import pallas as pl
from jax.experimental.pallas import tpu as pltpu
from jax.sharding import PartitionSpec as P

MESH = pl.DeviceIdType.MESH
CHUNKS = 4
BF16 = jnp.bfloat16
F32 = jnp.float32


def dot(a, b):
    return jnp.dot(a, b, preferred_element_type=F32)


def layout(blocks, capacity):
    slots = blocks * capacity
    left = slots - 16
    if left in (1, 2, 4, 8):
        return 16, left
    return -(-slots // 16) * 16, 0


def layer_kernel(
    dims,
    query_ref,
    key_hbm,
    value_hbm,
    new_key_ref,
    new_value_ref,
    length_ref,
    out_proj_hbm,
    residual_ref,
    gain_ref,
    id_ref,
    slot_ref,
    prob_ref,
    target_ref,
    unpack_ref,
    pack_ref,
    gate_hbm,
    up_hbm,
    down_hbm,
    stream_ref,
    moe_ref,
    keys,
    values,
    attn,
    out_proj,
    w_gate,
    w_up,
    w_down,
    sib_out,
    sib_in,
    part_out,
    part_in,
    table,
    tables,
    pick,
    spread,
    tokens,
    disp_out,
    disp_in,
    rows_in,
    gate_acc,
    up_acc,
    ret_out,
    ret_in,
    sum_out,
    sum_in,
    cache_sem,
    weight_sem,
    sib_sem,
    part_sem,
    table_sem,
    token_sem,
    disp_sem,
    ret_sem,
    sum_sem,
):
    R, K, full, left = dims["R"], dims["K"], dims["full"], dims["left"]
    top = dims["top"]
    M = 2 * K
    nch = CHUNKS
    width = stream_ref.shape[1]
    cw = width // nch
    parts = 16 // left if left else 0
    lw = cw // parts if left else 0
    s = lax.axis_index("sec")
    r = lax.axis_index("req")
    k = lax.axis_index("kv")
    m = s * K + k

    def cols(j):
        return pl.ds(pl.multiple_of(j * cw, cw), cw)

    def weight_copy(which, j):
        src, dst = [
            (out_proj_hbm.at[:, cols(j)], out_proj),
            (gate_hbm.at[0, cols(j)], w_gate),
            (up_hbm.at[0, cols(j)], w_up),
            (down_hbm.at[0, :, cols(j)], w_down),
        ][which]
        return pltpu.make_async_copy(src, dst.at[j], weight_sem.at[which, j])

    key_copy = pltpu.make_async_copy(key_hbm.at[:, 0], keys, cache_sem.at[0])
    value_copy = pltpu.make_async_copy(value_hbm.at[:, 0], values, cache_sem.at[1])
    key_copy.start()
    value_copy.start()
    for j in range(nch):
        weight_copy(0, j).start()

    def line(i):
        return lax.rem(r + i, R)

    def plane(i):
        return lax.rem(m + i, M)

    def remote(src, dst, sems, at, device):
        return pltpu.make_async_remote_copy(
            src_ref=src,
            dst_ref=dst,
            send_sem=sems.at[(0, *at)],
            recv_sem=sems.at[(1, *at)],
            device_id=device,
            device_id_type=MESH,
        )

    barrier = pltpu.get_barrier_semaphore()
    for i in range(1, M):
        p = plane(i)
        pl.semaphore_signal(
            barrier, inc=1, device_id=(p // K, r, lax.rem(p, K)), device_id_type=MESH
        )
    for i in range(1, R):
        pl.semaphore_signal(barrier, inc=1, device_id=(s, line(i), k), device_id_type=MESH)
    def table_copy(i, me):
        return remote(table, tables.at[me], table_sem, (i - 1,), (s, line(i), k))

    def sib_copy(j):
        return remote(sib_out.at[j, 1 - s], sib_in.at[j], sib_sem, (j,), (1 - s, r, k))

    def part_copy(j, i):
        to = lax.rem(k + i, K)
        return remote(
            part_out.at[j, to], part_in.at[j, i - 1], part_sem, (j, i - 1), (s, r, to)
        )

    def token_copy(j, i, me):
        return remote(tokens.at[j, me], tokens.at[j, me], token_sem, (j, i - 1), (s, line(i), k))

    def plane_copy(out, into, sems, j, i, me):
        p = plane(i)
        return remote(out.at[j, p], into.at[j, me], sems, (j, i - 1), (p // K, r, lax.rem(p, K)))

    def sum_copy(j, i):
        to = line(i)
        return remote(sum_out.at[j, to], sum_in.at[j, i - 1], sum_sem, (j, i - 1), (s, to, k))

    def before(i):
        return lax.rem(r - i + R, R)

    def plane_before(i):
        return lax.rem(m - i + M, M)

    code_scale = 1.0 * dims["capacity"]
    first_code = (r * (R * M * dims["capacity"])).astype(F32)
    codes_t = id_ref[...].astype(F32) * code_scale + slot_ref[...].astype(F32) + first_code
    probs_t = prob_ref[...]
    on_diagonal = lax.broadcasted_iota(jnp.int32, (16, 16), 0) == lax.broadcasted_iota(
        jnp.int32, (16, 16), 1
    )
    lane = lax.broadcasted_iota(jnp.int32, (16, 128), 1)
    filled = jnp.zeros((16, 128), F32)
    for n in range(top):
        for at, source in ((n, codes_t), (top + n, probs_t)):
            column = jnp.sum(
                jnp.where(on_diagonal, source[n : n + 1, :], 0.0), axis=1, keepdims=True
            )
            filled = jnp.where(lane == at, column, filled)
    table[...] = filled

    tokens_here = query_ref.shape[0]
    head = keys.shape[2]
    positions = keys.shape[1]
    heads = query_ref.shape[1] // head
    score_scale = 1.0 / head**0.5
    square = (tokens_here, tokens_here)
    length_column = jnp.sum(
        jnp.where(
            lax.broadcasted_iota(jnp.int32, square, 0) == lax.broadcasted_iota(jnp.int32, square, 1),
            length_ref[...].astype(F32),
            0.0,
        ),
        axis=1,
        keepdims=True,
    )
    query_rows = 16 * heads
    row_token = lax.broadcasted_iota(jnp.int32, (query_rows, 1), 0) % 16
    key_lane = lax.broadcasted_iota(jnp.int32, (1, 16 * positions), 1)
    same_token = key_lane // positions == row_token
    position = (key_lane % positions).astype(F32)
    own_token = lax.broadcasted_iota(jnp.int32, (1, 16), 1) == row_token
    key_copy.wait()
    value_copy.wait()
    for which in range(1, 4):
        for j in range(nch):
            weight_copy(which, j).start()

    def contract_last(a, b):
        return lax.dot_general(a, b, (((1,), (1,)), ((), ())), preferred_element_type=F32)

    for g in range(tokens_here // 16):
        at = slice(g * 16, (g + 1) * 16)
        query = jnp.concatenate(
            [query_ref[at, h * head : (h + 1) * head] for h in range(heads)], axis=0
        )
        limit = jnp.concatenate([length_column[at]] * heads, axis=0)
        score = contract_last(query, keys[at].reshape(16 * positions, head)) * score_scale
        own = contract_last(query, new_key_ref[at, :]) * score_scale
        score = jnp.where(same_token & (position < limit), score, -jnp.inf)
        own = jnp.where(own_token, own, -jnp.inf)
        highest = jnp.maximum(
            jnp.max(score, axis=1, keepdims=True), jnp.max(own, axis=1, keepdims=True)
        )
        score = jnp.exp(score - highest)
        own = jnp.exp(own - highest)
        total = jnp.sum(score, axis=1, keepdims=True) + jnp.sum(own, axis=1, keepdims=True)
        score = (score / total).astype(BF16)
        own = (own / total).astype(BF16)
        mixed = dot(score, values[at].reshape(16 * positions, head)) + dot(
            own, new_value_ref[at, :]
        )
        mixed = mixed.astype(BF16)
        for h in range(heads):
            attn[at, h * head : (h + 1) * head] = mixed[h * 16 : (h + 1) * 16]

    pl.semaphore_wait(barrier, M + R - 2)
    for i in range(1, R):
        table_copy(i, r).start()
    tables[r] = filled

    @pl.loop(0, nch)
    def _(j):
        weight_copy(0, j).wait()
        sib_out[j] = dot(attn[...], out_proj[j]).astype(BF16).reshape(2, K * 16, cw)
        sib_copy(j).start()

    @pl.loop(0, nch)
    def _(j):
        sib_copy(j).wait_recv()
        part_out[j] = (sib_out[j, s].astype(F32) + sib_in[j].astype(F32)).astype(BF16).reshape(K, 16, cw)
        for i in range(1, K):
            part_copy(j, i).start()

    for i in range(1, R):
        table_copy(i, before(i)).wait_recv()
    shift = (r * (K * dims["capacity"])).astype(F32)

    def routes(q, targets):
        chosen = jnp.zeros((16, targets.shape[1]), F32)
        weights = jnp.zeros((16, targets.shape[1]), F32)
        entry = tables[q]
        for n in range(top):
            hit = entry[:, n : n + 1] == targets
            chosen = jnp.where(hit, 1.0, chosen)
            weights = jnp.where(hit, entry[:, top + n : top + n + 1], weights)
        return chosen, weights

    for n in range(1 + parts):
        targets = target_ref[n : n + 1, :] + shift
        chosen = []
        for q in range(R):
            hits, weights = routes(q, targets)
            chosen.append(hits)
            spread[n, q * 16 : (q + 1) * 16, :] = weights.astype(BF16)
        pick[n] = jnp.concatenate(chosen, axis=0).T.astype(BF16)

    def add_parts(j, squares):
        total = part_out[j, k].astype(F32)
        for i in range(1, K):
            part_copy(j, i).wait_recv()
            total = total + part_in[j, i - 1].astype(F32)
        value = (residual_ref[:, cols(j)].astype(F32) + total).astype(BF16)
        stream_ref[:, cols(j)] = value
        value = value.astype(F32)
        return squares + jnp.sum(value * value, axis=1, keepdims=True)

    squares = lax.fori_loop(0, nch, add_parts, jnp.zeros((16, 1), F32))
    scale = lax.rsqrt(squares * (1.0 / width) + 1e-06)

    @pl.loop(0, nch)
    def _(j):
        value = stream_ref[:, cols(j)].astype(F32)
        tokens[j, r] = (value * scale * gain_ref[:, cols(j)]).astype(BF16)
        for i in range(1, R):
            token_copy(j, i, r).start()

    @pl.loop(0, nch)
    def _(j):
        for i in range(1, R):
            token_copy(j, i, before(i)).wait_recv()
        held = tokens[j].reshape(R * 16, cw)
        disp_out[j, :, :, 0:cw] = dot(pick[0], held).astype(BF16).reshape(M, full, cw)
        if left:
            extra = dot(pick[1], held[:, 0:lw])
            for q in range(1, parts):
                extra = extra + dot(pick[1 + q], held[:, q * lw : (q + 1) * lw])
            disp_out[j, :, :, cw : cw + lw] = extra.astype(BF16).reshape(M, 16, lw)
        for i in range(1, M):
            plane_copy(disp_out, disp_in, disp_sem, j, i, m).start()
        disp_in[j, m] = disp_out[j, m]

    gate_acc[...] = jnp.zeros_like(gate_acc)
    up_acc[...] = jnp.zeros_like(up_acc)

    @pl.loop(0, nch)
    def _(j):
        weight_copy(1, j).wait()
        weight_copy(2, j).wait()
        for i in range(1, M):
            plane_copy(disp_out, disp_in, disp_sem, j, i, plane_before(i)).wait_recv()
        rows_in[0 : M * full, :] = disp_in[j, :, :, 0:cw].reshape(M * full, cw)
        if left:
            extra = disp_in[j, :, :, cw : cw + lw].reshape(M * 16, lw)
            for q in range(parts):
                rows_in[M * full :, q * lw : (q + 1) * lw] = dot(unpack_ref[q], extra).astype(BF16)
        gate_acc[...] += dot(rows_in[...], w_gate[j])
        up_acc[...] += dot(rows_in[...], w_up[j])

    gate_out = gate_acc[...]
    hidden = (gate_out / (1.0 + jnp.exp(-gate_out)) * up_acc[...]).astype(BF16)

    @pl.loop(0, nch)
    def _(j):
        weight_copy(3, j).wait()
        finished = dot(hidden, w_down[j]).astype(BF16)
        ret_out[j, :, :, 0:cw] = finished[0 : M * full].reshape(M, full, cw)
        if left:
            rest = finished[M * full :]
            extra = dot(pack_ref[0], rest[:, 0:lw])
            for q in range(1, parts):
                extra = extra + dot(pack_ref[q], rest[:, q * lw : (q + 1) * lw])
            ret_out[j, :, :, cw : cw + lw] = extra.astype(BF16).reshape(M, 16, lw)
        for i in range(1, M):
            plane_copy(ret_out, ret_in, ret_sem, j, i, m).start()
        ret_in[j, m] = ret_out[j, m]

    @pl.loop(0, nch)
    def _(j):
        for i in range(1, M):
            plane_copy(ret_out, ret_in, ret_sem, j, i, plane_before(i)).wait_recv()
        total = dot(spread[0], ret_in[j, :, :, 0:cw].reshape(M * full, cw))
        if left:
            extra = ret_in[j, :, :, cw : cw + lw].reshape(M * 16, lw)
            total = total + jnp.concatenate(
                [dot(spread[1 + q], extra) for q in range(parts)], axis=1
            )
        sum_out[j] = total.astype(BF16).reshape(R, 16, cw)
        for i in range(1, R):
            sum_copy(j, i).start()

    @pl.loop(0, nch)
    def _(j):
        total = sum_out[j, r].astype(F32)
        for i in range(1, R):
            sum_copy(j, i).wait_recv()
            total = total + sum_in[j, i - 1].astype(F32)
        moe_ref[:, cols(j)] = total.astype(BF16)

    for i in range(1, R):
        table_copy(i, r).wait_send()

    @pl.loop(0, nch)
    def _(j):
        sib_copy(j).wait_send()
        for i in range(1, K):
            part_copy(j, i).wait_send()
        for i in range(1, R):
            token_copy(j, i, r).wait_send()
            sum_copy(j, i).wait_send()
        for i in range(1, M):
            plane_copy(disp_out, disp_in, disp_sem, j, i, m).wait_send()
            plane_copy(ret_out, ret_in, ret_sem, j, i, m).wait_send()


def hand_over(stream_ref, moe_ref, stream_out, moe_out, sems):
    copies = [
        pltpu.make_async_copy(stream_ref, stream_out, sems.at[0]),
        pltpu.make_async_copy(moe_ref, moe_out, sems.at[1]),
    ]
    for copy in copies:
        copy.start()
    for copy in copies:
        copy.wait()


def on_device(
    queries,
    key_cache,
    value_cache,
    new_keys,
    new_values,
    lengths,
    out_proj,
    residual,
    norm_gain,
    expert_ids,
    expert_slots,
    gate_probs,
    w_gate,
    w_up,
    w_down,
):
    R, K = lax.axis_size("req"), lax.axis_size("kv")
    M = 2 * K
    experts = R * M
    block, top = expert_ids.shape
    width = out_proj.shape[1]
    depth = out_proj.shape[0]
    hidden_units = w_gate.shape[2]
    capacity = top * block // experts + 1
    full, left = layout(R, capacity)
    parts = 16 // left if left else 1
    nch = CHUNKS
    cw = width // nch
    total_width = cw + (cw // parts if left else 0)
    row_count, _, positions, head = key_cache.shape

    member = np.arange(M)
    base = ((member // K) * R * K + member % K) * capacity
    slot = np.arange(full)
    code_of = (slot // capacity) * (experts * capacity) + slot % capacity
    targets = base[:, None] + np.where(slot < R * capacity, code_of, -(10**6))[None, :]
    targets = targets.reshape(-1).astype(np.float32)
    left_targets = np.full((parts, M, 16), -(10.0**6), np.float32)
    unpack = np.zeros((parts, M * max(left, 1), M * 16), np.float32)
    for q in range(parts if left else 0):
        for n in range(left):
            sigma = full + n
            code = (sigma // capacity) * (experts * capacity) + sigma % capacity
            left_targets[q, :, q * left + n] = base + code
            unpack[q, member * left + n, member * 16 + q * left + n] = 1.0
    targets = targets.reshape(1, -1)
    if left:
        targets = np.concatenate([targets, left_targets.reshape(parts, M * 16)], axis=0)

    rows = M * (full + left)
    dims = {"R": R, "K": K, "full": full, "left": left, "top": top, "capacity": capacity}
    vmem = pl.BlockSpec(memory_space=pltpu.VMEM)
    hbm = pl.BlockSpec(memory_space=pl.ANY)
    dma = pltpu.SemaphoreType.DMA
    outs = jax.ShapeDtypeStruct((block, width), BF16)
    stream, moe_out = pl.pallas_call(
        functools.partial(layer_kernel, dims),
        out_shape=(outs, outs),
        in_specs=[vmem, hbm, hbm] + [vmem] * 3 + [hbm] + [vmem] * 8 + [hbm] * 3,
        out_specs=(vmem, vmem),
        scratch_shapes=[
            pltpu.VMEM((row_count, positions, head), BF16),
            pltpu.VMEM((row_count, positions, head), BF16),
            pltpu.VMEM((row_count, depth), BF16),
            pltpu.VMEM((nch, depth, cw), BF16),
            pltpu.VMEM((nch, cw, hidden_units), BF16),
            pltpu.VMEM((nch, cw, hidden_units), BF16),
            pltpu.VMEM((nch, hidden_units, cw), BF16),
            pltpu.VMEM((nch, 2, K * block, cw), BF16),
            pltpu.VMEM((nch, K * block, cw), BF16),
            pltpu.VMEM((nch, K, block, cw), BF16),
            pltpu.VMEM((nch, K - 1, block, cw), BF16),
            pltpu.VMEM((block, 128), F32),
            pltpu.VMEM((R, block, 128), F32),
            pltpu.VMEM((len(targets), M * full, R * block), BF16),
            pltpu.VMEM((len(targets), R * block, M * full), BF16),
            pltpu.VMEM((nch, R, block, cw), BF16),
            pltpu.VMEM((nch, M, full, total_width), BF16),
            pltpu.VMEM((nch, M, full, total_width), BF16),
            pltpu.VMEM((rows, cw), BF16),
            pltpu.VMEM((rows, hidden_units), F32),
            pltpu.VMEM((rows, hidden_units), F32),
            pltpu.VMEM((nch, M, full, total_width), BF16),
            pltpu.VMEM((nch, M, full, total_width), BF16),
            pltpu.VMEM((nch, R, block, cw), BF16),
            pltpu.VMEM((nch, R - 1, block, cw), BF16),
            dma((2,)),
            dma((4, nch)),
            dma((2, nch)),
            dma((2, nch, K - 1)),
            dma((2, R - 1)),
            dma((2, nch, R - 1)),
            dma((2, nch, M - 1)),
            dma((2, nch, M - 1)),
            dma((2, nch, R - 1)),
        ],
        compiler_params=pltpu.CompilerParams(
            collective_id=0, has_side_effects=True, vmem_limit_bytes=58 * 2**20
        ),
    )(
        queries,
        key_cache,
        value_cache,
        new_keys[:, 0],
        new_values[:, 0],
        lengths.reshape(1, row_count),
        out_proj,
        residual,
        norm_gain.reshape(1, width),
        expert_ids.T,
        expert_slots.T,
        gate_probs.T,
        jnp.asarray(targets),
        jnp.asarray(unpack, BF16),
        jnp.asarray(unpack.transpose(0, 2, 1), BF16),
        w_gate,
        w_up,
        w_down,
    )
    return pl.pallas_call(
        hand_over,
        out_shape=(outs, outs),
        in_specs=[hbm, hbm],
        out_specs=(hbm, hbm),
        scratch_shapes=[dma((2,))],
    )(stream, moe_out)


def solution(mesh):
    return jax.shard_map(
        on_device,
        mesh=mesh,
        in_specs=(
            P("req", ("kv", "sec")),
            P("req", "kv", None, None),
            P("req", "kv", None, None),
            P("req", "kv", None),
            P("req", "kv", None),
            P("req"),
            P(("kv", "sec"), None),
            P(("req", "sec", "kv"), None),
            P(),
            P(("req", "sec", "kv"), None),
            P(("req", "sec", "kv"), None),
            P(("req", "sec", "kv"), None),
            P(("sec", "req", "kv"), None, None),
            P(("sec", "req", "kv"), None, None),
            P(("sec", "req", "kv"), None, None),
        ),
        out_specs=(P(("req", "sec", "kv"), None), P(("req", "sec", "kv"), None)),
        check_vma=False,
    )
```

```python
import functools

import jax
import jax.numpy as jnp
import numpy as np
from jax import lax
from jax.experimental import pallas as pl
from jax.experimental.pallas import tpu as pltpu
from jax.sharding import PartitionSpec as P

MESH = pl.DeviceIdType.MESH
CHUNKS = 8
BF16 = jnp.bfloat16
F32 = jnp.float32


def dot(a, b):
    return jnp.dot(a, b, preferred_element_type=F32)


def layout(blocks, capacity):
    slots = blocks * capacity
    left = slots - 16
    if left in (1, 2, 4, 8):
        return 16, left
    return -(-slots // 16) * 16, 0


def layer_kernel(
    dims,
    query_ref,
    key_hbm,
    value_hbm,
    new_key_ref,
    new_value_ref,
    length_ref,
    out_proj_hbm,
    residual_ref,
    gain_ref,
    id_ref,
    slot_ref,
    prob_ref,
    target_ref,
    unpack_ref,
    pack_ref,
    gate_hbm,
    up_hbm,
    down_hbm,
    stream_ref,
    moe_ref,
    keys,
    values,
    attn,
    out_proj,
    w_gate,
    w_up,
    w_down,
    sib_out,
    sib_in,
    part_out,
    part_in,
    table,
    tables,
    pick,
    spread,
    tokens,
    disp_out,
    disp_in,
    rows_in,
    gate_acc,
    up_acc,
    ret_out,
    ret_in,
    sum_out,
    sum_in,
    cache_sem,
    weight_sem,
    sib_sem,
    part_sem,
    table_sem,
    token_sem,
    disp_sem,
    ret_sem,
    sum_sem,
):
    R, K, full, left = dims["R"], dims["K"], dims["full"], dims["left"]
    top = dims["top"]
    M = 2 * K
    nch = CHUNKS
    width = stream_ref.shape[1]
    cw = width // nch
    parts = 16 // left if left else 0
    lw = cw // parts if left else 0
    s = lax.axis_index("sec")
    r = lax.axis_index("req")
    k = lax.axis_index("kv")
    m = s * K + k

    def cols(j):
        return pl.ds(pl.multiple_of(j * cw, cw), cw)

    def weight_copy(which, j):
        src, dst = [
            (out_proj_hbm.at[:, cols(j)], out_proj),
            (gate_hbm.at[0, cols(j)], w_gate),
            (up_hbm.at[0, cols(j)], w_up),
            (down_hbm.at[0, :, cols(j)], w_down),
        ][which]
        return pltpu.make_async_copy(src, dst.at[j], weight_sem.at[which, j])

    key_copy = pltpu.make_async_copy(key_hbm.at[:, 0], keys, cache_sem.at[0])
    value_copy = pltpu.make_async_copy(value_hbm.at[:, 0], values, cache_sem.at[1])
    key_copy.start()
    value_copy.start()
    for j in range(nch):
        weight_copy(0, j).start()

    def line(i):
        return lax.rem(r + i, R)

    def plane(i):
        return lax.rem(m + i, M)

    def remote(src, dst, sems, at, device):
        return pltpu.make_async_remote_copy(
            src_ref=src,
            dst_ref=dst,
            send_sem=sems.at[(0, *at)],
            recv_sem=sems.at[(1, *at)],
            device_id=device,
            device_id_type=MESH,
        )

    barrier = pltpu.get_barrier_semaphore()
    for i in range(1, M):
        p = plane(i)
        pl.semaphore_signal(
            barrier, inc=1, device_id=(p // K, r, lax.rem(p, K)), device_id_type=MESH
        )
    for i in range(1, R):
        pl.semaphore_signal(barrier, inc=1, device_id=(s, line(i), k), device_id_type=MESH)
    def table_copy(i, me):
        return remote(table, tables.at[me], table_sem, (i - 1,), (s, line(i), k))

    def sib_copy(j):
        return remote(sib_out.at[j, 1 - s], sib_in.at[j], sib_sem, (j,), (1 - s, r, k))

    def part_copy(j, i):
        to = lax.rem(k + i, K)
        return remote(
            part_out.at[j, to], part_in.at[j, i - 1], part_sem, (j, i - 1), (s, r, to)
        )

    def token_copy(j, i, me):
        return remote(tokens.at[j, me], tokens.at[j, me], token_sem, (j, i - 1), (s, line(i), k))

    def plane_copy(out, into, sems, j, i, me):
        p = plane(i)
        return remote(out.at[j, p], into.at[j, me], sems, (j, i - 1), (p // K, r, lax.rem(p, K)))

    def sum_copy(j, i):
        to = line(i)
        return remote(sum_out.at[j, to], sum_in.at[j, i - 1], sum_sem, (j, i - 1), (s, to, k))

    def before(i):
        return lax.rem(r - i + R, R)

    def plane_before(i):
        return lax.rem(m - i + M, M)

    code_scale = 1.0 * dims["capacity"]
    first_code = (r * (R * M * dims["capacity"])).astype(F32)
    codes_t = id_ref[...].astype(F32) * code_scale + slot_ref[...].astype(F32) + first_code
    probs_t = prob_ref[...]
    on_diagonal = lax.broadcasted_iota(jnp.int32, (16, 16), 0) == lax.broadcasted_iota(
        jnp.int32, (16, 16), 1
    )
    lane = lax.broadcasted_iota(jnp.int32, (16, 128), 1)
    filled = jnp.zeros((16, 128), F32)
    for n in range(top):
        for at, source in ((n, codes_t), (top + n, probs_t)):
            column = jnp.sum(
                jnp.where(on_diagonal, source[n : n + 1, :], 0.0), axis=1, keepdims=True
            )
            filled = jnp.where(lane == at, column, filled)
    table[...] = filled

    tokens_here = query_ref.shape[0]
    head = keys.shape[2]
    positions = keys.shape[1]
    heads = query_ref.shape[1] // head
    score_scale = 1.0 / head**0.5
    square = (tokens_here, tokens_here)
    length_column = jnp.sum(
        jnp.where(
            lax.broadcasted_iota(jnp.int32, square, 0) == lax.broadcasted_iota(jnp.int32, square, 1),
            length_ref[...].astype(F32),
            0.0,
        ),
        axis=1,
        keepdims=True,
    )
    query_rows = 16 * heads
    row_token = lax.broadcasted_iota(jnp.int32, (query_rows, 1), 0) % 16
    key_lane = lax.broadcasted_iota(jnp.int32, (1, 16 * positions), 1)
    same_token = key_lane // positions == row_token
    position = (key_lane % positions).astype(F32)
    own_token = lax.broadcasted_iota(jnp.int32, (1, 16), 1) == row_token
    key_copy.wait()
    value_copy.wait()
    for which in range(1, 4):
        for j in range(nch):
            weight_copy(which, j).start()

    def contract_last(a, b):
        return lax.dot_general(a, b, (((1,), (1,)), ((), ())), preferred_element_type=F32)

    for g in range(tokens_here // 16):
        at = slice(g * 16, (g + 1) * 16)
        query = jnp.concatenate(
            [query_ref[at, h * head : (h + 1) * head] for h in range(heads)], axis=0
        )
        limit = jnp.concatenate([length_column[at]] * heads, axis=0)
        score = contract_last(query, keys[at].reshape(16 * positions, head)) * score_scale
        own = contract_last(query, new_key_ref[at, :]) * score_scale
        score = jnp.where(same_token & (position < limit), score, -jnp.inf)
        own = jnp.where(own_token, own, -jnp.inf)
        highest = jnp.maximum(
            jnp.max(score, axis=1, keepdims=True), jnp.max(own, axis=1, keepdims=True)
        )
        score = jnp.exp(score - highest)
        own = jnp.exp(own - highest)
        total = jnp.sum(score, axis=1, keepdims=True) + jnp.sum(own, axis=1, keepdims=True)
        score = (score / total).astype(BF16)
        own = (own / total).astype(BF16)
        mixed = dot(score, values[at].reshape(16 * positions, head)) + dot(
            own, new_value_ref[at, :]
        )
        mixed = mixed.astype(BF16)
        for h in range(heads):
            attn[at, h * head : (h + 1) * head] = mixed[h * 16 : (h + 1) * 16]

    pl.semaphore_wait(barrier, M + R - 2)
    for i in range(1, R):
        table_copy(i, r).start()
    tables[r] = filled

    @pl.loop(0, nch)
    def _(j):
        weight_copy(0, j).wait()
        sib_out[j] = dot(attn[...], out_proj[j]).astype(BF16).reshape(2, K * 16, cw)
        sib_copy(j).start()

    @pl.loop(0, nch)
    def _(j):
        sib_copy(j).wait_recv()
        part_out[j] = (sib_out[j, s].astype(F32) + sib_in[j].astype(F32)).astype(BF16).reshape(K, 16, cw)
        for i in range(1, K):
            part_copy(j, i).start()

    for i in range(1, R):
        table_copy(i, before(i)).wait_recv()
    shift = (r * (K * dims["capacity"])).astype(F32)

    def routes(q, targets):
        chosen = jnp.zeros((16, targets.shape[1]), F32)
        weights = jnp.zeros((16, targets.shape[1]), F32)
        entry = tables[q]
        for n in range(top):
            hit = entry[:, n : n + 1] == targets
            chosen = jnp.where(hit, 1.0, chosen)
            weights = jnp.where(hit, entry[:, top + n : top + n + 1], weights)
        return chosen, weights

    for n in range(1 + parts):
        targets = target_ref[n : n + 1, :] + shift
        chosen = []
        for q in range(R):
            hits, weights = routes(q, targets)
            chosen.append(hits)
            spread[n, q * 16 : (q + 1) * 16, :] = weights.astype(BF16)
        pick[n] = jnp.concatenate(chosen, axis=0).T.astype(BF16)

    def add_parts(j, squares):
        total = part_out[j, k].astype(F32)
        for i in range(1, K):
            part_copy(j, i).wait_recv()
            total = total + part_in[j, i - 1].astype(F32)
        value = (residual_ref[:, cols(j)].astype(F32) + total).astype(BF16)
        stream_ref[:, cols(j)] = value
        value = value.astype(F32)
        return squares + jnp.sum(value * value, axis=1, keepdims=True)

    squares = lax.fori_loop(0, nch, add_parts, jnp.zeros((16, 1), F32))
    scale = lax.rsqrt(squares * (1.0 / width) + 1e-06)

    @pl.loop(0, nch)
    def _(j):
        value = stream_ref[:, cols(j)].astype(F32)
        tokens[j, r] = (value * scale * gain_ref[:, cols(j)]).astype(BF16)
        for i in range(1, R):
            token_copy(j, i, r).start()

    @pl.loop(0, nch)
    def _(j):
        for i in range(1, R):
            token_copy(j, i, before(i)).wait_recv()
        held = tokens[j].reshape(R * 16, cw)
        disp_out[j, :, :, 0:cw] = dot(pick[0], held).astype(BF16).reshape(M, full, cw)
        if left:
            extra = dot(pick[1], held[:, 0:lw])
            for q in range(1, parts):
                extra = extra + dot(pick[1 + q], held[:, q * lw : (q + 1) * lw])
            disp_out[j, :, :, cw : cw + lw] = extra.astype(BF16).reshape(M, 16, lw)
        for i in range(1, M):
            plane_copy(disp_out, disp_in, disp_sem, j, i, m).start()
        disp_in[j, m] = disp_out[j, m]

    gate_acc[...] = jnp.zeros_like(gate_acc)
    up_acc[...] = jnp.zeros_like(up_acc)

    @pl.loop(0, nch)
    def _(j):
        weight_copy(1, j).wait()
        weight_copy(2, j).wait()
        for i in range(1, M):
            plane_copy(disp_out, disp_in, disp_sem, j, i, plane_before(i)).wait_recv()
        rows_in[0 : M * full, :] = disp_in[j, :, :, 0:cw].reshape(M * full, cw)
        if left:
            extra = disp_in[j, :, :, cw : cw + lw].reshape(M * 16, lw)
            for q in range(parts):
                rows_in[M * full :, q * lw : (q + 1) * lw] = dot(unpack_ref[q], extra).astype(BF16)
        gate_acc[...] += dot(rows_in[...], w_gate[j])
        up_acc[...] += dot(rows_in[...], w_up[j])

    gate_out = gate_acc[...]
    hidden = (gate_out / (1.0 + jnp.exp(-gate_out)) * up_acc[...]).astype(BF16)

    @pl.loop(0, nch)
    def _(j):
        weight_copy(3, j).wait()
        finished = dot(hidden, w_down[j]).astype(BF16)
        ret_out[j, :, :, 0:cw] = finished[0 : M * full].reshape(M, full, cw)
        if left:
            rest = finished[M * full :]
            extra = dot(pack_ref[0], rest[:, 0:lw])
            for q in range(1, parts):
                extra = extra + dot(pack_ref[q], rest[:, q * lw : (q + 1) * lw])
            ret_out[j, :, :, cw : cw + lw] = extra.astype(BF16).reshape(M, 16, lw)
        for i in range(1, M):
            plane_copy(ret_out, ret_in, ret_sem, j, i, m).start()
        ret_in[j, m] = ret_out[j, m]

    @pl.loop(0, nch)
    def _(j):
        for i in range(1, M):
            plane_copy(ret_out, ret_in, ret_sem, j, i, plane_before(i)).wait_recv()
        total = dot(spread[0], ret_in[j, :, :, 0:cw].reshape(M * full, cw))
        if left:
            extra = ret_in[j, :, :, cw : cw + lw].reshape(M * 16, lw)
            total = total + jnp.concatenate(
                [dot(spread[1 + q], extra) for q in range(parts)], axis=1
            )
        sum_out[j] = total.astype(BF16).reshape(R, 16, cw)
        for i in range(1, R):
            sum_copy(j, i).start()

    @pl.loop(0, nch)
    def _(j):
        total = sum_out[j, r].astype(F32)
        for i in range(1, R):
            sum_copy(j, i).wait_recv()
            total = total + sum_in[j, i - 1].astype(F32)
        moe_ref[:, cols(j)] = total.astype(BF16)

    for i in range(1, R):
        table_copy(i, r).wait_send()

    @pl.loop(0, nch)
    def _(j):
        sib_copy(j).wait_send()
        for i in range(1, K):
            part_copy(j, i).wait_send()
        for i in range(1, R):
            token_copy(j, i, r).wait_send()
            sum_copy(j, i).wait_send()
        for i in range(1, M):
            plane_copy(disp_out, disp_in, disp_sem, j, i, m).wait_send()
            plane_copy(ret_out, ret_in, ret_sem, j, i, m).wait_send()


def hand_over(stream_ref, moe_ref, stream_out, moe_out):
    stream_out[...] = stream_ref[...]
    moe_out[...] = moe_ref[...]


def on_device(
    queries,
    key_cache,
    value_cache,
    new_keys,
    new_values,
    lengths,
    out_proj,
    residual,
    norm_gain,
    expert_ids,
    expert_slots,
    gate_probs,
    w_gate,
    w_up,
    w_down,
):
    R, K = lax.axis_size("req"), lax.axis_size("kv")
    M = 2 * K
    experts = R * M
    block, top = expert_ids.shape
    width = out_proj.shape[1]
    depth = out_proj.shape[0]
    hidden_units = w_gate.shape[2]
    capacity = top * block // experts + 1
    full, left = layout(R, capacity)
    parts = 16 // left if left else 1
    nch = CHUNKS
    cw = width // nch
    total_width = cw + (cw // parts if left else 0)
    row_count, _, positions, head = key_cache.shape

    member = np.arange(M)
    base = ((member // K) * R * K + member % K) * capacity
    slot = np.arange(full)
    code_of = (slot // capacity) * (experts * capacity) + slot % capacity
    targets = base[:, None] + np.where(slot < R * capacity, code_of, -(10**6))[None, :]
    targets = targets.reshape(-1).astype(np.float32)
    left_targets = np.full((parts, M, 16), -(10.0**6), np.float32)
    unpack = np.zeros((parts, M * max(left, 1), M * 16), np.float32)
    for q in range(parts if left else 0):
        for n in range(left):
            sigma = full + n
            code = (sigma // capacity) * (experts * capacity) + sigma % capacity
            left_targets[q, :, q * left + n] = base + code
            unpack[q, member * left + n, member * 16 + q * left + n] = 1.0
    targets = targets.reshape(1, -1)
    if left:
        targets = np.concatenate([targets, left_targets.reshape(parts, M * 16)], axis=0)

    rows = M * (full + left)
    dims = {"R": R, "K": K, "full": full, "left": left, "top": top, "capacity": capacity}
    vmem = pl.BlockSpec(memory_space=pltpu.VMEM)
    hbm = pl.BlockSpec(memory_space=pl.ANY)
    dma = pltpu.SemaphoreType.DMA
    outs = jax.ShapeDtypeStruct((block, width), BF16)
    stream, moe_out = pl.pallas_call(
        functools.partial(layer_kernel, dims),
        out_shape=(outs, outs),
        in_specs=[vmem, hbm, hbm] + [vmem] * 3 + [hbm] + [vmem] * 8 + [hbm] * 3,
        out_specs=(vmem, vmem),
        scratch_shapes=[
            pltpu.VMEM((row_count, positions, head), BF16),
            pltpu.VMEM((row_count, positions, head), BF16),
            pltpu.VMEM((row_count, depth), BF16),
            pltpu.VMEM((nch, depth, cw), BF16),
            pltpu.VMEM((nch, cw, hidden_units), BF16),
            pltpu.VMEM((nch, cw, hidden_units), BF16),
            pltpu.VMEM((nch, hidden_units, cw), BF16),
            pltpu.VMEM((nch, 2, K * block, cw), BF16),
            pltpu.VMEM((nch, K * block, cw), BF16),
            pltpu.VMEM((nch, K, block, cw), BF16),
            pltpu.VMEM((nch, K - 1, block, cw), BF16),
            pltpu.VMEM((block, 128), F32),
            pltpu.VMEM((R, block, 128), F32),
            pltpu.VMEM((len(targets), M * full, R * block), BF16),
            pltpu.VMEM((len(targets), R * block, M * full), BF16),
            pltpu.VMEM((nch, R, block, cw), BF16),
            pltpu.VMEM((nch, M, full, total_width), BF16),
            pltpu.VMEM((nch, M, full, total_width), BF16),
            pltpu.VMEM((rows, cw), BF16),
            pltpu.VMEM((rows, hidden_units), F32),
            pltpu.VMEM((rows, hidden_units), F32),
            pltpu.VMEM((nch, M, full, total_width), BF16),
            pltpu.VMEM((nch, M, full, total_width), BF16),
            pltpu.VMEM((nch, R, block, cw), BF16),
            pltpu.VMEM((nch, R - 1, block, cw), BF16),
            dma((2,)),
            dma((4, nch)),
            dma((2, nch)),
            dma((2, nch, K - 1)),
            dma((2, R - 1)),
            dma((2, nch, R - 1)),
            dma((2, nch, M - 1)),
            dma((2, nch, M - 1)),
            dma((2, nch, R - 1)),
        ],
        compiler_params=pltpu.CompilerParams(
            collective_id=0, has_side_effects=True, vmem_limit_bytes=58 * 2**20
        ),
    )(
        queries,
        key_cache,
        value_cache,
        new_keys[:, 0],
        new_values[:, 0],
        lengths.reshape(1, row_count),
        out_proj,
        residual,
        norm_gain.reshape(1, width),
        expert_ids.T,
        expert_slots.T,
        gate_probs.T,
        jnp.asarray(targets),
        jnp.asarray(unpack, BF16),
        jnp.asarray(unpack.transpose(0, 2, 1), BF16),
        w_gate,
        w_up,
        w_down,
    )
    return pl.pallas_call(
        hand_over,
        out_shape=(outs, outs),
        in_specs=[vmem, vmem],
        out_specs=(vmem, vmem),
    )(stream, moe_out)


def solution(mesh):
    return jax.shard_map(
        on_device,
        mesh=mesh,
        in_specs=(
            P("req", ("kv", "sec")),
            P("req", "kv", None, None),
            P("req", "kv", None, None),
            P("req", "kv", None),
            P("req", "kv", None),
            P("req"),
            P(("kv", "sec"), None),
            P(("req", "sec", "kv"), None),
            P(),
            P(("req", "sec", "kv"), None),
            P(("req", "sec", "kv"), None),
            P(("req", "sec", "kv"), None),
            P(("sec", "req", "kv"), None, None),
            P(("sec", "req", "kv"), None, None),
            P(("sec", "req", "kv"), None, None),
        ),
        out_specs=(P(("req", "sec", "kv"), None), P(("req", "sec", "kv"), None)),
        check_vma=False,
    )
```

```python
import functools

import jax
import jax.numpy as jnp
import numpy as np
from jax import lax
from jax.experimental import pallas as pl
from jax.experimental.pallas import tpu as pltpu
from jax.sharding import PartitionSpec as P

MESH = pl.DeviceIdType.MESH
CHUNKS = 8
BF16 = jnp.bfloat16
F32 = jnp.float32


def dot(a, b):
    return jnp.dot(a, b, preferred_element_type=F32)


def layout(blocks, capacity):
    slots = blocks * capacity
    left = slots - 16
    if left in (1, 2, 4, 8):
        return 16, left
    return -(-slots // 16) * 16, 0


def layer_kernel(
    dims,
    query_ref,
    key_hbm,
    value_hbm,
    new_key_ref,
    new_value_ref,
    length_ref,
    out_proj_hbm,
    residual_ref,
    gain_ref,
    id_ref,
    slot_ref,
    prob_ref,
    target_ref,
    unpack_ref,
    pack_ref,
    gate_hbm,
    up_hbm,
    down_hbm,
    stream_ref,
    moe_ref,
    keys,
    values,
    attn,
    out_proj,
    w_gate,
    w_up,
    w_down,
    sib_out,
    sib_in,
    part_out,
    part_in,
    table,
    tables,
    pick,
    spread,
    tokens,
    disp_out,
    disp_in,
    rows_in,
    gate_acc,
    up_acc,
    ret_out,
    ret_in,
    sum_out,
    sum_in,
    scales,
    slot_scale_out,
    slot_scale_in,
    row_scale,
    cache_sem,
    weight_sem,
    sib_sem,
    part_sem,
    table_sem,
    token_sem,
    disp_sem,
    ret_sem,
    sum_sem,
    scale_sem,
    slot_scale_sem,
):
    R, K, full, left = dims["R"], dims["K"], dims["full"], dims["left"]
    top = dims["top"]
    M = 2 * K
    nch = CHUNKS
    width = stream_ref.shape[1]
    cw = width // nch
    parts = 16 // left if left else 0
    lw = cw // parts if left else 0
    s = lax.axis_index("sec")
    r = lax.axis_index("req")
    k = lax.axis_index("kv")
    m = s * K + k

    def cols(j):
        return pl.ds(pl.multiple_of(j * cw, cw), cw)

    def weight_copy(which, j):
        src, dst = [
            (out_proj_hbm.at[:, cols(j)], out_proj),
            (gate_hbm.at[0, cols(j)], w_gate),
            (up_hbm.at[0, cols(j)], w_up),
            (down_hbm.at[0, :, cols(j)], w_down),
        ][which]
        return pltpu.make_async_copy(src, dst.at[j], weight_sem.at[which, j])

    key_copy = pltpu.make_async_copy(key_hbm.at[:, 0], keys, cache_sem.at[0])
    value_copy = pltpu.make_async_copy(value_hbm.at[:, 0], values, cache_sem.at[1])
    key_copy.start()
    value_copy.start()
    for j in range(nch):
        weight_copy(0, j).start()

    def line(i):
        return lax.rem(r + i, R)

    def plane(i):
        return lax.rem(m + i, M)

    def remote(src, dst, sems, at, device):
        return pltpu.make_async_remote_copy(
            src_ref=src,
            dst_ref=dst,
            send_sem=sems.at[(0, *at)],
            recv_sem=sems.at[(1, *at)],
            device_id=device,
            device_id_type=MESH,
        )

    barrier = pltpu.get_barrier_semaphore()
    for i in range(1, M):
        p = plane(i)
        pl.semaphore_signal(
            barrier, inc=1, device_id=(p // K, r, lax.rem(p, K)), device_id_type=MESH
        )
    for i in range(1, R):
        pl.semaphore_signal(barrier, inc=1, device_id=(s, line(i), k), device_id_type=MESH)
    def table_copy(i, me):
        return remote(table, tables.at[me], table_sem, (i - 1,), (s, line(i), k))

    def sib_copy(j):
        return remote(sib_out.at[j, 1 - s], sib_in.at[j], sib_sem, (j,), (1 - s, r, k))

    def part_copy(j, i):
        to = lax.rem(k + i, K)
        return remote(
            part_out.at[j, to], part_in.at[j, i - 1], part_sem, (j, i - 1), (s, r, to)
        )

    def token_copy(j, i, me):
        return remote(tokens.at[j, me], tokens.at[j, me], token_sem, (j, i - 1), (s, line(i), k))

    def plane_copy(out, into, sems, j, i, me):
        p = plane(i)
        return remote(out.at[j, p], into.at[j, me], sems, (j, i - 1), (p // K, r, lax.rem(p, K)))

    def sum_copy(j, i):
        to = line(i)
        return remote(sum_out.at[j, to], sum_in.at[j, i - 1], sum_sem, (j, i - 1), (s, to, k))

    def scale_copy(i, me):
        return remote(scales.at[me], scales.at[me], scale_sem, (i - 1,), (s, line(i), k))

    def slot_scale_copy(i, me):
        p = plane(i)
        return remote(
            slot_scale_out.at[p],
            slot_scale_in.at[me],
            slot_scale_sem,
            (i - 1,),
            (p // K, r, lax.rem(p, K)),
        )

    def before(i):
        return lax.rem(r - i + R, R)

    def plane_before(i):
        return lax.rem(m - i + M, M)

    code_scale = 1.0 * dims["capacity"]
    first_code = (r * (R * M * dims["capacity"])).astype(F32)
    codes_t = id_ref[...].astype(F32) * code_scale + slot_ref[...].astype(F32) + first_code
    probs_t = prob_ref[...]
    on_diagonal = lax.broadcasted_iota(jnp.int32, (16, 16), 0) == lax.broadcasted_iota(
        jnp.int32, (16, 16), 1
    )
    lane = lax.broadcasted_iota(jnp.int32, (16, 128), 1)
    filled = jnp.zeros((16, 128), F32)
    for n in range(top):
        for at, source in ((n, codes_t), (top + n, probs_t)):
            column = jnp.sum(
                jnp.where(on_diagonal, source[n : n + 1, :], 0.0), axis=1, keepdims=True
            )
            filled = jnp.where(lane == at, column, filled)
    table[...] = filled

    tokens_here = query_ref.shape[0]
    head = keys.shape[2]
    positions = keys.shape[1]
    heads = query_ref.shape[1] // head
    score_scale = 1.0 / head**0.5
    square = (tokens_here, tokens_here)
    length_column = jnp.sum(
        jnp.where(
            lax.broadcasted_iota(jnp.int32, square, 0) == lax.broadcasted_iota(jnp.int32, square, 1),
            length_ref[...].astype(F32),
            0.0,
        ),
        axis=1,
        keepdims=True,
    )
    query_rows = 16 * heads
    row_token = lax.broadcasted_iota(jnp.int32, (query_rows, 1), 0) % 16
    key_lane = lax.broadcasted_iota(jnp.int32, (1, 16 * positions), 1)
    same_token = key_lane // positions == row_token
    position = (key_lane % positions).astype(F32)
    own_token = lax.broadcasted_iota(jnp.int32, (1, 16), 1) == row_token
    key_copy.wait()
    value_copy.wait()
    for which in range(1, 4):
        for j in range(nch):
            weight_copy(which, j).start()

    def contract_last(a, b):
        return lax.dot_general(a, b, (((1,), (1,)), ((), ())), preferred_element_type=F32)

    for g in range(tokens_here // 16):
        at = slice(g * 16, (g + 1) * 16)
        query = jnp.concatenate(
            [query_ref[at, h * head : (h + 1) * head] for h in range(heads)], axis=0
        )
        limit = jnp.concatenate([length_column[at]] * heads, axis=0)
        score = contract_last(query, keys[at].reshape(16 * positions, head)) * score_scale
        own = contract_last(query, new_key_ref[at, :]) * score_scale
        score = jnp.where(same_token & (position < limit), score, -jnp.inf)
        own = jnp.where(own_token, own, -jnp.inf)
        highest = jnp.maximum(
            jnp.max(score, axis=1, keepdims=True), jnp.max(own, axis=1, keepdims=True)
        )
        score = jnp.exp(score - highest)
        own = jnp.exp(own - highest)
        total = jnp.sum(score, axis=1, keepdims=True) + jnp.sum(own, axis=1, keepdims=True)
        score = (score / total).astype(BF16)
        own = (own / total).astype(BF16)
        mixed = dot(score, values[at].reshape(16 * positions, head)) + dot(
            own, new_value_ref[at, :]
        )
        mixed = mixed.astype(BF16)
        for h in range(heads):
            attn[at, h * head : (h + 1) * head] = mixed[h * 16 : (h + 1) * 16]

    pl.semaphore_wait(barrier, M + R - 2)
    for i in range(1, R):
        table_copy(i, r).start()
    tables[r] = filled

    @pl.loop(0, nch)
    def _(j):
        weight_copy(0, j).wait()
        sib_out[j] = dot(attn[...], out_proj[j]).astype(BF16).reshape(2, K * 16, cw)
        sib_copy(j).start()

    @pl.loop(0, nch)
    def _(j):
        sib_copy(j).wait_recv()
        part_out[j] = (sib_out[j, s].astype(F32) + sib_in[j].astype(F32)).astype(BF16).reshape(K, 16, cw)
        for i in range(1, K):
            part_copy(j, i).start()

    for i in range(1, R):
        table_copy(i, before(i)).wait_recv()
    shift = (r * (K * dims["capacity"])).astype(F32)

    def routes(q, targets):
        chosen = jnp.zeros((16, targets.shape[1]), F32)
        weights = jnp.zeros((16, targets.shape[1]), F32)
        entry = tables[q]
        for n in range(top):
            hit = entry[:, n : n + 1] == targets
            chosen = jnp.where(hit, 1.0, chosen)
            weights = jnp.where(hit, entry[:, top + n : top + n + 1], weights)
        return chosen, weights

    for n in range(1 + parts):
        targets = target_ref[n : n + 1, :] + shift
        chosen = []
        for q in range(R):
            hits, weights = routes(q, targets)
            chosen.append(hits)
            spread[n, q * 16 : (q + 1) * 16, :] = weights.astype(BF16)
        pick[n] = jnp.concatenate(chosen, axis=0).T.astype(BF16)

    def add_parts(j, squares):
        total = part_out[j, k].astype(F32)
        for i in range(1, K):
            part_copy(j, i).wait_recv()
            total = total + part_in[j, i - 1].astype(F32)
        value = (residual_ref[:, cols(j)].astype(F32) + total).astype(BF16)
        stream_ref[:, cols(j)] = value
        value = value.astype(F32)
        tokens[j, r] = (value * gain_ref[:, cols(j)]).astype(BF16)
        for i in range(1, R):
            token_copy(j, i, r).start()
        return squares + jnp.sum(value * value, axis=1, keepdims=True)

    squares = lax.fori_loop(0, nch, add_parts, jnp.zeros((16, 1), F32))
    scale = lax.rsqrt(squares * (1.0 / width) + 1e-06)
    scales[r] = jnp.broadcast_to(scale, (16, 128))
    for i in range(1, R):
        scale_copy(i, r).start()

    @pl.loop(0, nch)
    def _(j):
        for i in range(1, R):
            token_copy(j, i, before(i)).wait_recv()
        held = tokens[j].reshape(R * 16, cw)
        disp_out[j, :, :, 0:cw] = dot(pick[0], held).astype(BF16).reshape(M, full, cw)
        if left:
            extra = dot(pick[1], held[:, 0:lw])
            for q in range(1, parts):
                extra = extra + dot(pick[1 + q], held[:, q * lw : (q + 1) * lw])
            disp_out[j, :, :, cw : cw + lw] = extra.astype(BF16).reshape(M, 16, lw)
        for i in range(1, M):
            plane_copy(disp_out, disp_in, disp_sem, j, i, m).start()
        disp_in[j, m] = disp_out[j, m]

    for i in range(1, R):
        scale_copy(i, before(i)).wait_recv()
    scale = scales[...].reshape(R * 16, 128)
    scale_high = scale.astype(BF16)
    scale_low = (scale - scale_high.astype(F32)).astype(BF16)

    def slot_scales(n):
        picked = dot(pick[n], scale_high) + dot(pick[n], scale_low)
        return picked.reshape(M, full, 128)

    slot_scale_out[:, 0:full, :] = slot_scales(0)
    slot_scale_out[:, full : full + 8, :] = (
        slot_scales(1)[:, 0:8, :] if left else jnp.zeros((M, 8, 128), F32)
    )
    for i in range(1, M):
        slot_scale_copy(i, m).start()
    slot_scale_in[m] = slot_scale_out[m]

    for i in range(1, R):
        table_copy(i, r).wait_send()
        scale_copy(i, r).wait_send()

    @pl.loop(0, nch)
    def _(j):
        sib_copy(j).wait_send()
        for i in range(1, K):
            part_copy(j, i).wait_send()
        for i in range(1, R):
            token_copy(j, i, r).wait_send()

    gate_acc[...] = jnp.zeros_like(gate_acc)
    up_acc[...] = jnp.zeros_like(up_acc)

    @pl.loop(0, nch)
    def _(j):
        weight_copy(1, j).wait()
        weight_copy(2, j).wait()
        for i in range(1, M):
            plane_copy(disp_out, disp_in, disp_sem, j, i, plane_before(i)).wait_recv()
        rows_in[0 : M * full, :] = disp_in[j, :, :, 0:cw].reshape(M * full, cw)
        if left:
            extra = disp_in[j, :, :, cw : cw + lw].reshape(M * 16, lw)
            for q in range(parts):
                rows_in[M * full :, q * lw : (q + 1) * lw] = dot(unpack_ref[q], extra).astype(BF16)
        gate_acc[...] += dot(rows_in[...], w_gate[j])
        up_acc[...] += dot(rows_in[...], w_up[j])

    for i in range(1, M):
        slot_scale_copy(i, plane_before(i)).wait_recv()
    row_scale[0 : M * full, :] = slot_scale_in[:, 0:full, :].reshape(M * full, 128)
    if left:
        for p in range(M):
            at = M * full + p * left
            row_scale[at : at + left, :] = slot_scale_in[p, full : full + left, :]
    row_factor = row_scale[:, 0:1]
    gate_out = gate_acc[...] * row_factor
    up_out = up_acc[...] * row_factor
    hidden = (gate_out / (1.0 + jnp.exp(-gate_out)) * up_out).astype(BF16)

    @pl.loop(0, nch)
    def _(j):
        weight_copy(3, j).wait()
        finished = dot(hidden, w_down[j]).astype(BF16)
        ret_out[j, :, :, 0:cw] = finished[0 : M * full].reshape(M, full, cw)
        if left:
            rest = finished[M * full :]
            extra = dot(pack_ref[0], rest[:, 0:lw])
            for q in range(1, parts):
                extra = extra + dot(pack_ref[q], rest[:, q * lw : (q + 1) * lw])
            ret_out[j, :, :, cw : cw + lw] = extra.astype(BF16).reshape(M, 16, lw)
        for i in range(1, M):
            plane_copy(ret_out, ret_in, ret_sem, j, i, m).start()
        ret_in[j, m] = ret_out[j, m]

    for i in range(1, M):
        slot_scale_copy(i, m).wait_send()

    @pl.loop(0, nch)
    def _(j):
        for i in range(1, M):
            plane_copy(disp_out, disp_in, disp_sem, j, i, m).wait_send()

    @pl.loop(0, nch)
    def _(j):
        for i in range(1, M):
            plane_copy(ret_out, ret_in, ret_sem, j, i, plane_before(i)).wait_recv()
        total = dot(spread[0], ret_in[j, :, :, 0:cw].reshape(M * full, cw))
        if left:
            extra = ret_in[j, :, :, cw : cw + lw].reshape(M * 16, lw)
            total = total + jnp.concatenate(
                [dot(spread[1 + q], extra) for q in range(parts)], axis=1
            )
        sum_out[j] = total.astype(BF16).reshape(R, 16, cw)
        for i in range(1, R):
            sum_copy(j, i).start()

    @pl.loop(0, nch)
    def _(j):
        for i in range(1, M):
            plane_copy(ret_out, ret_in, ret_sem, j, i, m).wait_send()

    @pl.loop(0, nch)
    def _(j):
        total = sum_out[j, r].astype(F32)
        for i in range(1, R):
            sum_copy(j, i).wait_recv()
            total = total + sum_in[j, i - 1].astype(F32)
        moe_ref[:, cols(j)] = total.astype(BF16)
        for i in range(1, R):
            sum_copy(j, i).wait_send()


def hand_over(stream_ref, moe_ref, stream_out, moe_out):
    stream_out[...] = stream_ref[...]
    moe_out[...] = moe_ref[...]


def on_device(
    queries,
    key_cache,
    value_cache,
    new_keys,
    new_values,
    lengths,
    out_proj,
    residual,
    norm_gain,
    expert_ids,
    expert_slots,
    gate_probs,
    w_gate,
    w_up,
    w_down,
):
    R, K = lax.axis_size("req"), lax.axis_size("kv")
    M = 2 * K
    experts = R * M
    block, top = expert_ids.shape
    width = out_proj.shape[1]
    depth = out_proj.shape[0]
    hidden_units = w_gate.shape[2]
    capacity = top * block // experts + 1
    full, left = layout(R, capacity)
    parts = 16 // left if left else 1
    nch = CHUNKS
    cw = width // nch
    total_width = cw + (cw // parts if left else 0)
    row_count, _, positions, head = key_cache.shape

    member = np.arange(M)
    base = ((member // K) * R * K + member % K) * capacity
    slot = np.arange(full)
    code_of = (slot // capacity) * (experts * capacity) + slot % capacity
    targets = base[:, None] + np.where(slot < R * capacity, code_of, -(10**6))[None, :]
    targets = targets.reshape(-1).astype(np.float32)
    left_targets = np.full((parts, M, 16), -(10.0**6), np.float32)
    unpack = np.zeros((parts, M * max(left, 1), M * 16), np.float32)
    for q in range(parts if left else 0):
        for n in range(left):
            sigma = full + n
            code = (sigma // capacity) * (experts * capacity) + sigma % capacity
            left_targets[q, :, q * left + n] = base + code
            unpack[q, member * left + n, member * 16 + q * left + n] = 1.0
    targets = targets.reshape(1, -1)
    if left:
        targets = np.concatenate([targets, left_targets.reshape(parts, M * 16)], axis=0)

    rows = M * (full + left)
    dims = {"R": R, "K": K, "full": full, "left": left, "top": top, "capacity": capacity}
    vmem = pl.BlockSpec(memory_space=pltpu.VMEM)
    hbm = pl.BlockSpec(memory_space=pl.ANY)
    dma = pltpu.SemaphoreType.DMA
    outs = jax.ShapeDtypeStruct((block, width), BF16)
    stream, moe_out = pl.pallas_call(
        functools.partial(layer_kernel, dims),
        out_shape=(outs, outs),
        in_specs=[vmem, hbm, hbm] + [vmem] * 3 + [hbm] + [vmem] * 8 + [hbm] * 3,
        out_specs=(vmem, vmem),
        scratch_shapes=[
            pltpu.VMEM((row_count, positions, head), BF16),
            pltpu.VMEM((row_count, positions, head), BF16),
            pltpu.VMEM((row_count, depth), BF16),
            pltpu.VMEM((nch, depth, cw), BF16),
            pltpu.VMEM((nch, cw, hidden_units), BF16),
            pltpu.VMEM((nch, cw, hidden_units), BF16),
            pltpu.VMEM((nch, hidden_units, cw), BF16),
            pltpu.VMEM((nch, 2, K * block, cw), BF16),
            pltpu.VMEM((nch, K * block, cw), BF16),
            pltpu.VMEM((nch, K, block, cw), BF16),
            pltpu.VMEM((nch, K - 1, block, cw), BF16),
            pltpu.VMEM((block, 128), F32),
            pltpu.VMEM((R, block, 128), F32),
            pltpu.VMEM((len(targets), M * full, R * block), BF16),
            pltpu.VMEM((len(targets), R * block, M * full), BF16),
            pltpu.VMEM((nch, R, block, cw), BF16),
            pltpu.VMEM((nch, M, full, total_width), BF16),
            pltpu.VMEM((nch, M, full, total_width), BF16),
            pltpu.VMEM((rows, cw), BF16),
            pltpu.VMEM((rows, hidden_units), F32),
            pltpu.VMEM((rows, hidden_units), F32),
            pltpu.VMEM((nch, M, full, total_width), BF16),
            pltpu.VMEM((nch, M, full, total_width), BF16),
            pltpu.VMEM((nch, R, block, cw), BF16),
            pltpu.VMEM((nch, R - 1, block, cw), BF16),
            pltpu.VMEM((R, block, 128), F32),
            pltpu.VMEM((M, full + 8, 128), F32),
            pltpu.VMEM((M, full + 8, 128), F32),
            pltpu.VMEM((rows, 128), F32),
            dma((2,)),
            dma((4, nch)),
            dma((2, nch)),
            dma((2, nch, K - 1)),
            dma((2, R - 1)),
            dma((2, nch, R - 1)),
            dma((2, nch, M - 1)),
            dma((2, nch, M - 1)),
            dma((2, nch, R - 1)),
            dma((2, R - 1)),
            dma((2, M - 1)),
        ],
        compiler_params=pltpu.CompilerParams(
            collective_id=0, has_side_effects=True, vmem_limit_bytes=58 * 2**20
        ),
    )(
        queries,
        key_cache,
        value_cache,
        new_keys[:, 0],
        new_values[:, 0],
        lengths.reshape(1, row_count),
        out_proj,
        residual,
        norm_gain.reshape(1, width),
        expert_ids.T,
        expert_slots.T,
        gate_probs.T,
        jnp.asarray(targets),
        jnp.asarray(unpack, BF16),
        jnp.asarray(unpack.transpose(0, 2, 1), BF16),
        w_gate,
        w_up,
        w_down,
    )
    return pl.pallas_call(
        hand_over,
        out_shape=(outs, outs),
        in_specs=[vmem, vmem],
        out_specs=(vmem, vmem),
    )(stream, moe_out)


def solution(mesh):
    return jax.shard_map(
        on_device,
        mesh=mesh,
        in_specs=(
            P("req", ("kv", "sec")),
            P("req", "kv", None, None),
            P("req", "kv", None, None),
            P("req", "kv", None),
            P("req", "kv", None),
            P("req"),
            P(("kv", "sec"), None),
            P(("req", "sec", "kv"), None),
            P(),
            P(("req", "sec", "kv"), None),
            P(("req", "sec", "kv"), None),
            P(("req", "sec", "kv"), None),
            P(("sec", "req", "kv"), None, None),
            P(("sec", "req", "kv"), None, None),
            P(("sec", "req", "kv"), None, None),
        ),
        out_specs=(P(("req", "sec", "kv"), None), P(("req", "sec", "kv"), None)),
        check_vma=False,
    )
```

```python
import functools

import jax
import jax.numpy as jnp
import numpy as np
from jax import lax
from jax.experimental import pallas as pl
from jax.experimental.pallas import tpu as pltpu
from jax.sharding import PartitionSpec as P

MESH = pl.DeviceIdType.MESH
CHUNKS = 8
LAG = 2
BF16 = jnp.bfloat16
F32 = jnp.float32


def dot(a, b):
    return jnp.dot(a, b, preferred_element_type=F32)


def layout(blocks, capacity):
    slots = blocks * capacity
    left = slots - 16
    if left in (1, 2, 4, 8):
        return 16, left
    return -(-slots // 16) * 16, 0


def layer_kernel(
    dims,
    query_ref,
    key_hbm,
    value_hbm,
    new_key_ref,
    new_value_ref,
    length_ref,
    out_proj_hbm,
    residual_ref,
    gain_ref,
    id_ref,
    slot_ref,
    prob_ref,
    target_ref,
    unpack_ref,
    pack_ref,
    gate_hbm,
    up_hbm,
    down_hbm,
    stream_ref,
    moe_ref,
    keys,
    values,
    attn,
    out_proj,
    w_gate,
    w_up,
    w_down,
    sib_out,
    sib_in,
    part_out,
    part_in,
    table,
    tables,
    pick,
    spread,
    tokens,
    disp_out,
    disp_in,
    rows_in,
    gate_acc,
    up_acc,
    ret_out,
    ret_in,
    sum_out,
    sum_in,
    scales,
    slot_scale_out,
    slot_scale_in,
    row_scale,
    squares,
    cache_sem,
    weight_sem,
    sib_sem,
    part_sem,
    table_sem,
    token_sem,
    disp_sem,
    ret_sem,
    sum_sem,
    scale_sem,
    slot_scale_sem,
):
    R, K, full, left = dims["R"], dims["K"], dims["full"], dims["left"]
    top = dims["top"]
    M = 2 * K
    nch = CHUNKS
    width = stream_ref.shape[1]
    cw = width // nch
    parts = 16 // left if left else 0
    lw = cw // parts if left else 0
    s = lax.axis_index("sec")
    r = lax.axis_index("req")
    k = lax.axis_index("kv")
    m = s * K + k

    def cols(j):
        return pl.ds(pl.multiple_of(j * cw, cw), cw)

    def weight_copy(which, j):
        src, dst = [
            (out_proj_hbm.at[:, cols(j)], out_proj),
            (gate_hbm.at[0, cols(j)], w_gate),
            (up_hbm.at[0, cols(j)], w_up),
            (down_hbm.at[0, :, cols(j)], w_down),
        ][which]
        return pltpu.make_async_copy(src, dst.at[j], weight_sem.at[which, j])

    key_copy = pltpu.make_async_copy(key_hbm.at[:, 0], keys, cache_sem.at[0])
    value_copy = pltpu.make_async_copy(value_hbm.at[:, 0], values, cache_sem.at[1])
    key_copy.start()
    value_copy.start()
    for j in range(nch):
        weight_copy(0, j).start()

    def line(i):
        return lax.rem(r + i, R)

    def plane(i):
        return lax.rem(m + i, M)

    def remote(src, dst, sems, at, device):
        return pltpu.make_async_remote_copy(
            src_ref=src,
            dst_ref=dst,
            send_sem=sems.at[(0, *at)],
            recv_sem=sems.at[(1, *at)],
            device_id=device,
            device_id_type=MESH,
        )

    barrier = pltpu.get_barrier_semaphore()
    for i in range(1, M):
        p = plane(i)
        pl.semaphore_signal(
            barrier, inc=1, device_id=(p // K, r, lax.rem(p, K)), device_id_type=MESH
        )
    for i in range(1, R):
        pl.semaphore_signal(barrier, inc=1, device_id=(s, line(i), k), device_id_type=MESH)
    def table_copy(i, me):
        return remote(table, tables.at[me], table_sem, (i - 1,), (s, line(i), k))

    def sib_copy(j):
        return remote(sib_out.at[j, 1 - s], sib_in.at[j], sib_sem, (j,), (1 - s, r, k))

    def part_copy(j, i):
        to = lax.rem(k + i, K)
        return remote(
            part_out.at[j, to], part_in.at[j, i - 1], part_sem, (j, i - 1), (s, r, to)
        )

    def token_copy(j, i, me):
        return remote(tokens.at[j, me], tokens.at[j, me], token_sem, (j, i - 1), (s, line(i), k))

    def plane_copy(out, into, sems, j, i, me):
        p = plane(i)
        return remote(out.at[j, p], into.at[j, me], sems, (j, i - 1), (p // K, r, lax.rem(p, K)))

    def sum_copy(j, i):
        to = line(i)
        return remote(sum_out.at[j, to], sum_in.at[j, i - 1], sum_sem, (j, i - 1), (s, to, k))

    def scale_copy(i, me):
        return remote(scales.at[me], scales.at[me], scale_sem, (i - 1,), (s, line(i), k))

    def slot_scale_copy(i, me):
        p = plane(i)
        return remote(
            slot_scale_out.at[p],
            slot_scale_in.at[me],
            slot_scale_sem,
            (i - 1,),
            (p // K, r, lax.rem(p, K)),
        )

    def before(i):
        return lax.rem(r - i + R, R)

    def plane_before(i):
        return lax.rem(m - i + M, M)

    code_scale = 1.0 * dims["capacity"]
    first_code = (r * (R * M * dims["capacity"])).astype(F32)
    codes_t = id_ref[...].astype(F32) * code_scale + slot_ref[...].astype(F32) + first_code
    probs_t = prob_ref[...]
    on_diagonal = lax.broadcasted_iota(jnp.int32, (16, 16), 0) == lax.broadcasted_iota(
        jnp.int32, (16, 16), 1
    )
    lane = lax.broadcasted_iota(jnp.int32, (16, 128), 1)
    filled = jnp.zeros((16, 128), F32)
    for n in range(top):
        for at, source in ((n, codes_t), (top + n, probs_t)):
            column = jnp.sum(
                jnp.where(on_diagonal, source[n : n + 1, :], 0.0), axis=1, keepdims=True
            )
            filled = jnp.where(lane == at, column, filled)
    table[...] = filled

    tokens_here = query_ref.shape[0]
    head = keys.shape[2]
    positions = keys.shape[1]
    heads = query_ref.shape[1] // head
    score_scale = 1.0 / head**0.5
    square = (tokens_here, tokens_here)
    length_column = jnp.sum(
        jnp.where(
            lax.broadcasted_iota(jnp.int32, square, 0) == lax.broadcasted_iota(jnp.int32, square, 1),
            length_ref[...].astype(F32),
            0.0,
        ),
        axis=1,
        keepdims=True,
    )
    query_rows = 16 * heads
    row_token = lax.broadcasted_iota(jnp.int32, (query_rows, 1), 0) % 16
    key_lane = lax.broadcasted_iota(jnp.int32, (1, 16 * positions), 1)
    same_token = key_lane // positions == row_token
    position = (key_lane % positions).astype(F32)
    own_token = lax.broadcasted_iota(jnp.int32, (1, 16), 1) == row_token
    key_copy.wait()
    value_copy.wait()
    for which in range(1, 4):
        for j in range(nch):
            weight_copy(which, j).start()

    def contract_last(a, b):
        return lax.dot_general(a, b, (((1,), (1,)), ((), ())), preferred_element_type=F32)

    for g in range(tokens_here // 16):
        at = slice(g * 16, (g + 1) * 16)
        query = jnp.concatenate(
            [query_ref[at, h * head : (h + 1) * head] for h in range(heads)], axis=0
        )
        limit = jnp.concatenate([length_column[at]] * heads, axis=0)
        score = contract_last(query, keys[at].reshape(16 * positions, head)) * score_scale
        own = contract_last(query, new_key_ref[at, :]) * score_scale
        score = jnp.where(same_token & (position < limit), score, -jnp.inf)
        own = jnp.where(own_token, own, -jnp.inf)
        highest = jnp.maximum(
            jnp.max(score, axis=1, keepdims=True), jnp.max(own, axis=1, keepdims=True)
        )
        score = jnp.exp(score - highest)
        own = jnp.exp(own - highest)
        total = jnp.sum(score, axis=1, keepdims=True) + jnp.sum(own, axis=1, keepdims=True)
        score = (score / total).astype(BF16)
        own = (own / total).astype(BF16)
        mixed = dot(score, values[at].reshape(16 * positions, head)) + dot(
            own, new_value_ref[at, :]
        )
        mixed = mixed.astype(BF16)
        for h in range(heads):
            attn[at, h * head : (h + 1) * head] = mixed[h * 16 : (h + 1) * 16]

    pl.semaphore_wait(barrier, M + R - 2)
    for i in range(1, R):
        table_copy(i, r).start()
    tables[r] = filled

    @pl.loop(0, nch)
    def _(j):
        weight_copy(0, j).wait()
        sib_out[j] = dot(attn[...], out_proj[j]).astype(BF16).reshape(2, K * 16, cw)
        sib_copy(j).start()

    @pl.loop(0, nch)
    def _(j):
        sib_copy(j).wait_recv()
        part_out[j] = (sib_out[j, s].astype(F32) + sib_in[j].astype(F32)).astype(BF16).reshape(K, 16, cw)
        for i in range(1, K):
            part_copy(j, i).start()

    for i in range(1, R):
        table_copy(i, before(i)).wait_recv()
    shift = (r * (K * dims["capacity"])).astype(F32)

    def routes(q, targets):
        chosen = jnp.zeros((16, targets.shape[1]), F32)
        weights = jnp.zeros((16, targets.shape[1]), F32)
        entry = tables[q]
        for n in range(top):
            hit = entry[:, n : n + 1] == targets
            chosen = jnp.where(hit, 1.0, chosen)
            weights = jnp.where(hit, entry[:, top + n : top + n + 1], weights)
        return chosen, weights

    for n in range(1 + parts):
        targets = target_ref[n : n + 1, :] + shift
        chosen = []
        for q in range(R):
            hits, weights = routes(q, targets)
            chosen.append(hits)
            spread[n, q * 16 : (q + 1) * 16, :] = weights.astype(BF16)
        pick[n] = jnp.concatenate(chosen, axis=0).T.astype(BF16)

    def add_parts(j):
        total = part_out[j, k].astype(F32)
        for i in range(1, K):
            part_copy(j, i).wait_recv()
            total = total + part_in[j, i - 1].astype(F32)
        value = (residual_ref[:, cols(j)].astype(F32) + total).astype(BF16)
        stream_ref[:, cols(j)] = value
        value = value.astype(F32)
        tokens[j, r] = (value * gain_ref[:, cols(j)]).astype(BF16)
        for i in range(1, R):
            token_copy(j, i, r).start()
        squares[...] += jnp.sum(value * value, axis=1, keepdims=True)

    def dispatch(j):
        for i in range(1, R):
            token_copy(j, i, before(i)).wait_recv()
        held = tokens[j].reshape(R * 16, cw)
        disp_out[j, :, :, 0:cw] = dot(pick[0], held).astype(BF16).reshape(M, full, cw)
        if left:
            extra = dot(pick[1], held[:, 0:lw])
            for q in range(1, parts):
                extra = extra + dot(pick[1 + q], held[:, q * lw : (q + 1) * lw])
            disp_out[j, :, :, cw : cw + lw] = extra.astype(BF16).reshape(M, 16, lw)
        for i in range(1, M):
            plane_copy(disp_out, disp_in, disp_sem, j, i, m).start()
        disp_in[j, m] = disp_out[j, m]

    squares[...] = jnp.zeros_like(squares)

    @pl.loop(0, nch + LAG)
    def _(j):
        @pl.when(j < nch)
        def _():
            add_parts(j)

        @pl.when(j == nch - 1)
        def _():
            scale = lax.rsqrt(squares[...] * (1.0 / width) + 1e-06)
            scales[r] = jnp.broadcast_to(scale, (16, 128))
            for i in range(1, R):
                scale_copy(i, r).start()

        @pl.when(j >= LAG)
        def _():
            dispatch(j - LAG)

    for i in range(1, R):
        scale_copy(i, before(i)).wait_recv()
    scale = scales[...].reshape(R * 16, 128)
    scale_high = scale.astype(BF16)
    scale_low = (scale - scale_high.astype(F32)).astype(BF16)

    def slot_scales(n):
        picked = dot(pick[n], scale_high) + dot(pick[n], scale_low)
        return picked.reshape(M, full, 128)

    slot_scale_out[:, 0:full, :] = slot_scales(0)
    slot_scale_out[:, full : full + 8, :] = (
        slot_scales(1)[:, 0:8, :] if left else jnp.zeros((M, 8, 128), F32)
    )
    for i in range(1, M):
        slot_scale_copy(i, m).start()
    slot_scale_in[m] = slot_scale_out[m]

    for i in range(1, R):
        table_copy(i, r).wait_send()
        scale_copy(i, r).wait_send()

    @pl.loop(0, nch)
    def _(j):
        sib_copy(j).wait_send()
        for i in range(1, K):
            part_copy(j, i).wait_send()
        for i in range(1, R):
            token_copy(j, i, r).wait_send()

    gate_acc[...] = jnp.zeros_like(gate_acc)
    up_acc[...] = jnp.zeros_like(up_acc)

    @pl.loop(0, nch)
    def _(j):
        weight_copy(1, j).wait()
        weight_copy(2, j).wait()
        for i in range(1, M):
            plane_copy(disp_out, disp_in, disp_sem, j, i, plane_before(i)).wait_recv()
        rows_in[0 : M * full, :] = disp_in[j, :, :, 0:cw].reshape(M * full, cw)
        if left:
            extra = disp_in[j, :, :, cw : cw + lw].reshape(M * 16, lw)
            for q in range(parts):
                rows_in[M * full :, q * lw : (q + 1) * lw] = dot(unpack_ref[q], extra).astype(BF16)
        gate_acc[...] += dot(rows_in[...], w_gate[j])
        up_acc[...] += dot(rows_in[...], w_up[j])

    for i in range(1, M):
        slot_scale_copy(i, plane_before(i)).wait_recv()
    row_scale[0 : M * full, :] = slot_scale_in[:, 0:full, :].reshape(M * full, 128)
    if left:
        for p in range(M):
            at = M * full + p * left
            row_scale[at : at + left, :] = slot_scale_in[p, full : full + left, :]
    row_factor = row_scale[:, 0:1]
    gate_out = gate_acc[...] * row_factor
    up_out = up_acc[...] * row_factor
    hidden = (gate_out / (1.0 + jnp.exp(-gate_out)) * up_out).astype(BF16)

    @pl.loop(0, nch)
    def _(j):
        weight_copy(3, j).wait()
        finished = dot(hidden, w_down[j]).astype(BF16)
        ret_out[j, :, :, 0:cw] = finished[0 : M * full].reshape(M, full, cw)
        if left:
            rest = finished[M * full :]
            extra = dot(pack_ref[0], rest[:, 0:lw])
            for q in range(1, parts):
                extra = extra + dot(pack_ref[q], rest[:, q * lw : (q + 1) * lw])
            ret_out[j, :, :, cw : cw + lw] = extra.astype(BF16).reshape(M, 16, lw)
        for i in range(1, M):
            plane_copy(ret_out, ret_in, ret_sem, j, i, m).start()
        ret_in[j, m] = ret_out[j, m]

    for i in range(1, M):
        slot_scale_copy(i, m).wait_send()

    @pl.loop(0, nch)
    def _(j):
        for i in range(1, M):
            plane_copy(disp_out, disp_in, disp_sem, j, i, m).wait_send()

    @pl.loop(0, nch)
    def _(j):
        for i in range(1, M):
            plane_copy(ret_out, ret_in, ret_sem, j, i, plane_before(i)).wait_recv()
        total = dot(spread[0], ret_in[j, :, :, 0:cw].reshape(M * full, cw))
        if left:
            extra = ret_in[j, :, :, cw : cw + lw].reshape(M * 16, lw)
            total = total + jnp.concatenate(
                [dot(spread[1 + q], extra) for q in range(parts)], axis=1
            )
        sum_out[j] = total.astype(BF16).reshape(R, 16, cw)
        for i in range(1, R):
            sum_copy(j, i).start()

    @pl.loop(0, nch)
    def _(j):
        for i in range(1, M):
            plane_copy(ret_out, ret_in, ret_sem, j, i, m).wait_send()

    @pl.loop(0, nch)
    def _(j):
        total = sum_out[j, r].astype(F32)
        for i in range(1, R):
            sum_copy(j, i).wait_recv()
            total = total + sum_in[j, i - 1].astype(F32)
        moe_ref[:, cols(j)] = total.astype(BF16)
        for i in range(1, R):
            sum_copy(j, i).wait_send()


def hand_over(stream_ref, moe_ref, stream_out, moe_out):
    stream_out[...] = stream_ref[...]
    moe_out[...] = moe_ref[...]


def on_device(
    queries,
    key_cache,
    value_cache,
    new_keys,
    new_values,
    lengths,
    out_proj,
    residual,
    norm_gain,
    expert_ids,
    expert_slots,
    gate_probs,
    w_gate,
    w_up,
    w_down,
):
    R, K = lax.axis_size("req"), lax.axis_size("kv")
    M = 2 * K
    experts = R * M
    block, top = expert_ids.shape
    width = out_proj.shape[1]
    depth = out_proj.shape[0]
    hidden_units = w_gate.shape[2]
    capacity = top * block // experts + 1
    full, left = layout(R, capacity)
    parts = 16 // left if left else 1
    nch = CHUNKS
    cw = width // nch
    total_width = cw + (cw // parts if left else 0)
    row_count, _, positions, head = key_cache.shape

    member = np.arange(M)
    base = ((member // K) * R * K + member % K) * capacity
    slot = np.arange(full)
    code_of = (slot // capacity) * (experts * capacity) + slot % capacity
    targets = base[:, None] + np.where(slot < R * capacity, code_of, -(10**6))[None, :]
    targets = targets.reshape(-1).astype(np.float32)
    left_targets = np.full((parts, M, 16), -(10.0**6), np.float32)
    unpack = np.zeros((parts, M * max(left, 1), M * 16), np.float32)
    for q in range(parts if left else 0):
        for n in range(left):
            sigma = full + n
            code = (sigma // capacity) * (experts * capacity) + sigma % capacity
            left_targets[q, :, q * left + n] = base + code
            unpack[q, member * left + n, member * 16 + q * left + n] = 1.0
    targets = targets.reshape(1, -1)
    if left:
        targets = np.concatenate([targets, left_targets.reshape(parts, M * 16)], axis=0)

    rows = M * (full + left)
    dims = {"R": R, "K": K, "full": full, "left": left, "top": top, "capacity": capacity}
    vmem = pl.BlockSpec(memory_space=pltpu.VMEM)
    hbm = pl.BlockSpec(memory_space=pl.ANY)
    dma = pltpu.SemaphoreType.DMA
    outs = jax.ShapeDtypeStruct((block, width), BF16)
    stream, moe_out = pl.pallas_call(
        functools.partial(layer_kernel, dims),
        out_shape=(outs, outs),
        in_specs=[vmem, hbm, hbm] + [vmem] * 3 + [hbm] + [vmem] * 8 + [hbm] * 3,
        out_specs=(vmem, vmem),
        scratch_shapes=[
            pltpu.VMEM((row_count, positions, head), BF16),
            pltpu.VMEM((row_count, positions, head), BF16),
            pltpu.VMEM((row_count, depth), BF16),
            pltpu.VMEM((nch, depth, cw), BF16),
            pltpu.VMEM((nch, cw, hidden_units), BF16),
            pltpu.VMEM((nch, cw, hidden_units), BF16),
            pltpu.VMEM((nch, hidden_units, cw), BF16),
            pltpu.VMEM((nch, 2, K * block, cw), BF16),
            pltpu.VMEM((nch, K * block, cw), BF16),
            pltpu.VMEM((nch, K, block, cw), BF16),
            pltpu.VMEM((nch, K - 1, block, cw), BF16),
            pltpu.VMEM((block, 128), F32),
            pltpu.VMEM((R, block, 128), F32),
            pltpu.VMEM((len(targets), M * full, R * block), BF16),
            pltpu.VMEM((len(targets), R * block, M * full), BF16),
            pltpu.VMEM((nch, R, block, cw), BF16),
            pltpu.VMEM((nch, M, full, total_width), BF16),
            pltpu.VMEM((nch, M, full, total_width), BF16),
            pltpu.VMEM((rows, cw), BF16),
            pltpu.VMEM((rows, hidden_units), F32),
            pltpu.VMEM((rows, hidden_units), F32),
            pltpu.VMEM((nch, M, full, total_width), BF16),
            pltpu.VMEM((nch, M, full, total_width), BF16),
            pltpu.VMEM((nch, R, block, cw), BF16),
            pltpu.VMEM((nch, R - 1, block, cw), BF16),
            pltpu.VMEM((R, block, 128), F32),
            pltpu.VMEM((M, full + 8, 128), F32),
            pltpu.VMEM((M, full + 8, 128), F32),
            pltpu.VMEM((rows, 128), F32),
            pltpu.VMEM((block, 1), F32),
            dma((2,)),
            dma((4, nch)),
            dma((2, nch)),
            dma((2, nch, K - 1)),
            dma((2, R - 1)),
            dma((2, nch, R - 1)),
            dma((2, nch, M - 1)),
            dma((2, nch, M - 1)),
            dma((2, nch, R - 1)),
            dma((2, R - 1)),
            dma((2, M - 1)),
        ],
        compiler_params=pltpu.CompilerParams(
            collective_id=0, has_side_effects=True, vmem_limit_bytes=58 * 2**20
        ),
    )(
        queries,
        key_cache,
        value_cache,
        new_keys[:, 0],
        new_values[:, 0],
        lengths.reshape(1, row_count),
        out_proj,
        residual,
        norm_gain.reshape(1, width),
        expert_ids.T,
        expert_slots.T,
        gate_probs.T,
        jnp.asarray(targets),
        jnp.asarray(unpack, BF16),
        jnp.asarray(unpack.transpose(0, 2, 1), BF16),
        w_gate,
        w_up,
        w_down,
    )
    return pl.pallas_call(
        hand_over,
        out_shape=(outs, outs),
        in_specs=[vmem, vmem],
        out_specs=(vmem, vmem),
    )(stream, moe_out)


def solution(mesh):
    return jax.shard_map(
        on_device,
        mesh=mesh,
        in_specs=(
            P("req", ("kv", "sec")),
            P("req", "kv", None, None),
            P("req", "kv", None, None),
            P("req", "kv", None),
            P("req", "kv", None),
            P("req"),
            P(("kv", "sec"), None),
            P(("req", "sec", "kv"), None),
            P(),
            P(("req", "sec", "kv"), None),
            P(("req", "sec", "kv"), None),
            P(("req", "sec", "kv"), None),
            P(("sec", "req", "kv"), None, None),
            P(("sec", "req", "kv"), None, None),
            P(("sec", "req", "kv"), None, None),
        ),
        out_specs=(P(("req", "sec", "kv"), None), P(("req", "sec", "kv"), None)),
        check_vma=False,
    )
```
